256 devices in a mesh: grp: 8 (over y, core), seq: 32 (over x, z).
Axes of the slice: x: 4, y: 4, z: 8, core: 2. Of those that a mesh axis runs over, the one named last changes fastest.
Arguments:
- video_stream: bfloat16 [8, 32, 256, 1024], P('grp', 'seq'), may hold values from -6 to 6
- video_qkv: bfloat16 [8, 32, 256, 3072], P('grp', 'seq'), may hold values from -6 to 6
- out_weight: bfloat16 [1024, 1024], P(('grp', 'seq')), may hold values from -0.1875 to 0.1875
- text_states: bfloat16 [8, 16384, 3584], P('grp', 'seq'), may hold values from -6 to 6
- query_weight: bfloat16 [3584, 1024], P(('grp', 'seq')), may hold values from -0.09375 to 0.09375
- kv_weight: bfloat16 [1024, 2048], P(('grp', 'seq')), may hold values from -0.1875 to 0.1875
- read_weight: float32 [1024], replicated, may hold values from -0.75 to 0.75
- block_mask: int32 [8, 32, 3], P('grp', 'seq'), may hold values from 0 to 1, as said below
- pair_labels: int32 [8, 32], P('grp', 'seq'), may hold values from 0 to 1
Outputs:
- rewards: float32 [8, 32], P('grp', 'seq')
- loss: float32 [], replicated
- kv_grad: float32 [1024, 2048], P(('grp', 'seq'))
The draws below stay inside these ranges and needn't reach their ends.
Inputs may be any that keep to these rules, and one draw needn't show every extreme that they name: `block_mask`: column 1 is always 1; column 0 is 0 for segment 0 and column 2 is 0 for segment 32 - 1.
All inputs are finite; a program needn't handle non-finite values.
Results may differ from the reference program's by a relative error of at most 0.0075.
Values may be sent and summed in bfloat16 or wider, within the bound.
A program may use at most 128 MiB of HBM per device.

```python
import jax
import jax.numpy as jnp
from jax import lax

D = 1024
HEADS = 16
TW = 3584
P_SIZE = 256
TS = 512
ROWS = 256
FRAMES = 32
GROUPS = 8
SEGS = 32
TEXT = 16384


def draw_block_mask(key, part):
    key = jax.random.fold_in(key, 7)
    shape = (GROUPS, SEGS, 3)
    mask_bits = jax.random.randint(key, shape, 0, 2)
    segment = lax.broadcasted_iota(jnp.int32, shape, 1)
    column = lax.broadcasted_iota(jnp.int32, shape, 2)
    mask_bits = jnp.where(column == 1, 1, mask_bits)
    mask_bits = jnp.where((column == 0) & (segment == 0), 0, mask_bits)
    mask_bits = jnp.where((column == 2) & (segment == SEGS - 1), 0, mask_bits)
    return mask_bits.astype(jnp.int32)


def with_ends(entries, rng, smallest, largest):
    dims = entries.shape
    index_at = [jax.random.randint(jax.random.fold_in(rng, axis), (), 0, dims[axis]) for axis in range(len(dims))]
    entries = entries.at[tuple(index_at)].set(smallest)
    longest = dims.index(max(dims))
    index_at[longest] = (index_at[longest] + 1) % dims[longest]
    return entries.at[tuple(index_at)].set(largest)


def steps_of(rng, dims, cuts, least, largest):
    def one(position, blocks):
        steps = jax.random.uniform(jax.random.fold_in(jax.random.fold_in(rng, 6), position), (blocks,), jnp.float32, least / len(cuts), largest / len(cuts))
        return jnp.repeat(jnp.exp(steps), dims[position] // blocks).reshape((-1,) + (1,) * (len(dims) - position - 1))

    level = one(*cuts[0])
    for cut in cuts[1:]:
        level = level * one(*cut)
    return level


def scatter_about(rng, shape, scale, reach, cuts=(), kind=jnp.bfloat16):
    entries = jax.random.normal(rng, shape, jnp.float32) * scale
    if len(cuts) > 0:
        entries = steps_of(rng, shape, cuts, -0.22, 0.18) * entries
    return jnp.clip(entries, min=-reach, max=reach).astype(kind)


def setup_inputs(seed: int = 0) -> dict:
    streams_of = jax.random.split(jax.random.key(seed), 10)
    return {
        "video_stream": scatter_about(streams_of[0], (GROUPS, FRAMES, P_SIZE, D), 1.0, 6.0, ((0, 8), (1, 32))),
        "video_qkv": scatter_about(streams_of[1], (GROUPS, FRAMES, P_SIZE, 3 * D), 1.0, 6.0, ((0, 8), (1, 32))),
        "out_weight": scatter_about(streams_of[2], (D, D), D ** -0.5, 0.1875, ((0, 256),)),
        "text_states": scatter_about(streams_of[3], (GROUPS, TEXT, TW), 1.0, 6.0, ((0, 8), (1, 32))),
        "query_weight": scatter_about(streams_of[4], (TW, D), TW ** -0.5, 0.09375, ((0, 256),)),
        "kv_weight": scatter_about(streams_of[5], (D, 2 * D), D ** -0.5, 0.1875, ((0, 256),)),
        "read_weight": scatter_about(streams_of[6], (D,), (4.0 / D ** 0.5), 0.75, (), jnp.float32),
        "block_mask": draw_block_mask(jax.random.fold_in(streams_of[9], 71), 0),
        "pair_labels": with_ends(jax.random.randint(streams_of[8], (GROUPS, SEGS), 0, 2), jax.random.fold_in(streams_of[8], 1), 0, 1).astype(jnp.int32),
    }


epsilon = 1e-06

def attend_frames(video_block):
    frame_count, patch_count, _ = video_block.shape
    head_size = D // HEADS
    packed = video_block.astype(jnp.float32)
    queries = packed[..., :D].reshape(frame_count, patch_count, HEADS, head_size)
    keys = packed[..., D:2 * D].reshape(frame_count, patch_count, HEADS, head_size)
    values = packed[..., 2 * D:].reshape(frame_count, patch_count, HEADS, head_size)
    scores = jnp.einsum('fphd,gphd->phfg', queries, keys) * head_size ** (-0.5)
    probs = jax.nn.softmax(scores, axis=-1)
    probs_b = lax.optimization_barrier(probs.astype(jnp.bfloat16)).astype(jnp.float32)
    result = jnp.einsum('phfg,gphd->fphd', probs_b, values)
    return result.reshape(frame_count, patch_count, D).astype(jnp.bfloat16)

def cross_segment(query_rows, context_rows, context_kv, keep_mask, read_weight, label_value):
    head_size = D // HEADS
    scale = head_size ** (-0.5)
    token_count = query_rows.shape[0]
    key_count = context_kv.shape[0]
    query_heads = query_rows.astype(jnp.float32).reshape(token_count, HEADS, head_size)
    key_heads = context_kv[:, :D].astype(jnp.float32).reshape(key_count, HEADS, head_size)
    value_heads = context_kv[:, D:].astype(jnp.float32).reshape(key_count, HEADS, head_size)
    scores = jnp.einsum('thd,khd->htk', query_heads, key_heads) * scale
    scores = jnp.where(keep_mask[None, None, :], scores, -jnp.inf)
    probs = jax.nn.softmax(scores, axis=-1)
    probs_b = lax.optimization_barrier(probs.astype(jnp.bfloat16)).astype(jnp.float32)
    cross_out = jnp.einsum('htk,khd->thd', probs_b, value_heads).reshape(token_count, D)
    root_mean = jnp.sqrt(lax.optimization_barrier(jnp.mean(cross_out * cross_out, axis=-1, keepdims=True)) + epsilon)
    normed = cross_out / root_mean
    gates = jax.nn.sigmoid(normed)
    reward = jnp.mean(lax.optimization_barrier(jnp.sum(normed * gates * read_weight, axis=-1)))
    signed = 2.0 * label_value.astype(jnp.float32) - 1.0
    loss_value = jax.nn.softplus(-signed * reward)
    slope = -signed * jax.nn.sigmoid(-signed * reward) / (GROUPS * SEGS)
    d_normed = slope / token_count * read_weight * gates * (1.0 + normed * (1.0 - gates))
    d_out = (d_normed - normed * lax.optimization_barrier(jnp.mean(d_normed * normed, axis=-1, keepdims=True))) / root_mean
    d_out_b = lax.optimization_barrier(d_out.astype(jnp.bfloat16)).astype(jnp.float32)
    d_out_heads = d_out_b.reshape(token_count, HEADS, head_size)
    d_probs = jnp.einsum('thd,khd->htk', d_out_heads, value_heads)
    d_scores = probs * (d_probs - lax.optimization_barrier(jnp.sum(probs * d_probs, axis=-1, keepdims=True))) * scale
    d_scores_b = lax.optimization_barrier(d_scores.astype(jnp.bfloat16)).astype(jnp.float32)
    d_keys = jnp.einsum('htk,thd->khd', d_scores_b, query_heads).reshape(key_count, D)
    d_values = jnp.einsum('htk,thd->khd', probs_b, d_out_heads).reshape(key_count, D)
    d_kv = jnp.concatenate([d_keys, d_values], axis=1).astype(jnp.bfloat16)
    grad_term = jnp.dot(context_rows.T, d_kv, preferred_element_type=jnp.float32)
    return (reward, loss_value, grad_term)

def reference(video_stream, video_qkv, out_weight, text_states, query_weight, kv_weight, read_weight, block_mask, pair_labels):
    grad_total = jnp.zeros((D, 2 * D), jnp.float32)
    reward_list = []
    loss_list = []
    for group_index in range(GROUPS):
        stream_rows = video_stream[group_index].reshape(FRAMES * P_SIZE, D)
        temporal = attend_frames(video_qkv[group_index]).reshape(FRAMES * P_SIZE, D)
        mixed = (stream_rows.astype(jnp.float32) + jnp.dot(temporal, out_weight, preferred_element_type=jnp.float32)).astype(jnp.bfloat16)
        keys_values = jnp.dot(mixed, kv_weight, preferred_element_type=jnp.float32).astype(jnp.bfloat16)
        queries = jnp.dot(text_states[group_index], query_weight, preferred_element_type=jnp.float32).astype(jnp.bfloat16)
        mixed_padded = jnp.pad(mixed, ((ROWS, ROWS), (0, 0)))
        kv_padded = jnp.pad(keys_values, ((ROWS, ROWS), (0, 0)))
        group_masks = block_mask[group_index]
        group_labels = pair_labels[group_index]

        def segment_step(running, segment):
            first_row = (segment * ROWS).astype(jnp.int32)
            context_rows = lax.dynamic_slice_in_dim(mixed_padded, first_row, 3 * ROWS, 0)
            context_kv = lax.dynamic_slice_in_dim(kv_padded, first_row, 3 * ROWS, 0)
            query_rows = lax.dynamic_slice_in_dim(queries, (segment * TS).astype(jnp.int32), TS, 0)
            keep_mask = jnp.repeat(group_masks[segment], ROWS) == 1
            reward, loss_value, grad_term = cross_segment(query_rows, context_rows, context_kv, keep_mask, read_weight, group_labels[segment])
            return (running + grad_term, (reward, loss_value))
        grad_total, (group_rewards, group_losses) = lax.scan(segment_step, grad_total, jnp.arange(SEGS, dtype=jnp.int32))
        reward_list.append(group_rewards)
        loss_list.append(group_losses)
    rewards = jnp.stack(reward_list)
    loss = jnp.sum(jnp.stack(loss_list)) / (GROUPS * SEGS)
    return (rewards, loss, grad_total)
```

```python
import functools
import jax
import jax.numpy as jnp
from jax import lax
from jax.experimental import pallas as pl
from jax.experimental.pallas import tpu as pltpu
from jax.sharding import PartitionSpec as P

HEADS = 16
MESH = pl.DeviceIdType.MESH
EPSILON = 1e-06
NN = (((1,), (0,)), ((), ()))
NT = (((1,), (1,)), ((), ()))
VMEM = pl.BlockSpec(memory_space=pltpu.VMEM)
SMEM = pl.BlockSpec(memory_space=pltpu.SMEM)


def mm(a, b, dims=NN):
    return lax.dot_general(a, b, dims, preferred_element_type=jnp.float32)


def cross_kernel(
    pair_count, mask_ref, label_ref, q_ref, prev_ref, own_ref, next_ref, wkv_ref, read_ref,
    reward_ref, loss_ref, dkv_ref, kv, vt, exps, inverse, out_t, slopes, d_out_t, d_out,
):
    tokens, width = q_ref.shape
    rows = own_ref.shape[0]
    keys = 3 * rows
    pairs = width // 128
    blocks = [pl.ds(b * rows, rows) for b in range(3)]

    @pl.loop(0, 4)
    def _(c):
        cols = pl.ds(pl.multiple_of(c * (width // 2), 128), width // 2)
        w = wkv_ref[:, cols]
        for b, ref in enumerate((prev_ref, own_ref, next_ref)):
            kv[blocks[b], cols] = mm(ref[...], w).astype(jnp.bfloat16)

    lane = lax.broadcasted_iota(jnp.int32, (1, 128), 1)
    sides = [((lane // 64) == h).astype(jnp.bfloat16) for h in range(2)]
    bias = [jnp.where(mask_ref[b] == 1, 0.0, -jnp.inf).astype(jnp.float32) for b in range(3)]

    def forward(j, squares):
        cols = pl.ds(pl.multiple_of(j * 128, 128), 128)
        vcols = pl.ds(pl.multiple_of(width + j * 128, 128), 128)
        vt[cols, :] = kv[:, vcols].T
        k = kv[:, cols]
        q = q_ref[:, cols]
        for h in range(2):
            s = mm(k, q * sides[h], NT)
            s = [s[b * rows : (b + 1) * rows] for b in range(3)]
            top = [jnp.max(s[b], axis=0, keepdims=True) + bias[b] for b in range(3)]
            top = jnp.maximum(jnp.maximum(top[0], top[1]), top[2])
            total = jnp.zeros((1, tokens), jnp.float32)
            for b in range(3):
                e = jnp.exp(s[b] - (top - bias[b]))
                exps[2 * j + h, blocks[b], :] = e
                total = total + jnp.sum(e, axis=0, keepdims=True)
            inv = 1.0 / total
            inverse[2 * j + h] = jnp.broadcast_to(inv, (8, tokens))
            p = (exps[2 * j + h] * inv).astype(jnp.bfloat16)
            mine = pl.ds(pl.multiple_of(j * 128 + h * 64, 64), 64)
            o = mm(vt[mine, :], p)
            out_t[mine, :] = o
            squares = squares + jnp.sum(o * o, axis=0, keepdims=True)
        return squares

    squares = lax.fori_loop(0, pairs, forward, jnp.zeros((1, tokens), jnp.float32))
    inv_root = 1.0 / jnp.sqrt(squares / width + EPSILON)

    def rewards(j, carry):
        reward, inner = carry
        cols = pl.ds(pl.multiple_of(j * 128, 128), 128)
        normed = out_t[cols, :] * inv_root
        gates = jax.nn.sigmoid(normed)
        read = read_ref[cols, 0:1]
        scaled = read * gates
        slope = scaled * (1.0 + normed * (1.0 - gates))
        slopes[cols, :] = slope
        reward = reward + jnp.sum(scaled * normed, axis=0, keepdims=True)
        inner = inner + jnp.sum(slope * normed, axis=0, keepdims=True)
        return reward, inner

    zero = jnp.zeros((1, tokens), jnp.float32)
    reward, inner = lax.fori_loop(0, pairs, rewards, (zero, zero))
    reward = jnp.sum(reward, axis=1, keepdims=True) / tokens
    signed = 2.0 * label_ref[0].astype(jnp.float32) - 1.0
    x = -signed * reward
    loss = jnp.maximum(x, 0.0) + jnp.log1p(jnp.exp(-jnp.abs(x)))
    reward_ref[...] = jnp.broadcast_to(reward, reward_ref.shape)
    loss_ref[...] = jnp.broadcast_to(loss, loss_ref.shape)
    factor = -signed * jax.nn.sigmoid(x) / pair_count / tokens
    inner = inner / width

    @pl.loop(0, pairs)
    def _(j):
        cols = pl.ds(pl.multiple_of(j * 128, 128), 128)
        normed = out_t[cols, :] * inv_root
        d = ((slopes[cols, :] - normed * inner) * (inv_root * factor)).astype(jnp.bfloat16)
        d_out_t[cols, :] = d
        d_out[:, cols] = d.T

    @pl.loop(0, pairs)
    def _(j):
        cols = pl.ds(pl.multiple_of(j * 128, 128), 128)
        vcols = pl.ds(pl.multiple_of(width + j * 128, 128), 128)
        v = kv[:, vcols]
        q = q_ref[:, cols]
        do = d_out[:, cols]
        empty = jnp.zeros((64, tokens), jnp.bfloat16)
        dk = dv = None
        for h in range(2):
            mine = d_out_t[pl.ds(pl.multiple_of(j * 128 + h * 64, 64), 64), :]
            mine = jnp.concatenate([mine, empty] if h == 0 else [empty, mine], axis=0)
            dp = mm(v, mine)
            p = exps[2 * j + h] * inverse[2 * j + h, 0:1, :]
            both = p * dp
            ds = (both - p * jnp.sum(both, axis=0, keepdims=True)).astype(jnp.bfloat16)
            dkh = mm(ds, q * sides[h])
            dvh = mm(p.astype(jnp.bfloat16), do * sides[h])
            dk = dkh if dk is None else dk + dkh
            dv = dvh if dv is None else dv + dvh
        dkv_ref[:, cols] = dk.astype(jnp.bfloat16)
        dkv_ref[:, vcols] = dv.astype(jnp.bfloat16)


def cross(mask, label, q, prev, own, after, wkv, read, pair_count):
    tokens, width = q.shape
    keys = 3 * own.shape[0]
    f32, bf16 = jnp.float32, jnp.bfloat16
    return pl.pallas_call(
        functools.partial(cross_kernel, pair_count),
        out_shape=(
            jax.ShapeDtypeStruct((8, 128), f32),
            jax.ShapeDtypeStruct((8, 128), f32),
            jax.ShapeDtypeStruct((keys, 2 * width), bf16),
        ),
        in_specs=[SMEM, SMEM] + [VMEM] * 6,
        out_specs=(VMEM, VMEM, VMEM),
        scratch_shapes=[
            pltpu.VMEM((keys, 2 * width), bf16),
            pltpu.VMEM((width, keys), bf16),
            pltpu.VMEM((HEADS, keys, tokens), f32),
            pltpu.VMEM((HEADS, 8, tokens), f32),
            pltpu.VMEM((width, tokens), f32),
            pltpu.VMEM((width, tokens), f32),
            pltpu.VMEM((width, tokens), bf16),
            pltpu.VMEM((tokens, width), bf16),
        ],
        compiler_params=pltpu.CompilerParams(vmem_limit_bytes=60 * 2**20),
        name="cross",
    )(mask, label, q, prev, own, after, wkv, read)


def reduce_kernel(
    prev_ref, own_ref, next_ref, dkv_ref, loss_ref, grad_ref, total_ref,
    acc, core_out, core_in, a1_out, a1_in, b1_out, b1_in, a2_out, a2_in, b2_out, b2_in,
    a_sum, b_sum, a3_out, a3_in, b3_out, b3_in, z_out, z_in, l_out, l_in, send, recv,
):
    f32, bf16 = jnp.float32, jnp.bfloat16
    grp, seq = lax.axis_index("grp"), lax.axis_index("seq")
    y, core = grp // 2, grp % 2
    x, z = seq // 8, seq % 8
    rows = own_ref.shape[0]
    half = acc.shape[2] // 2
    quarter = half // 2

    def y_peer(d):
        return (((y + d) % 4) * 2 + core, seq)

    def x_peer(d):
        return (grp, ((x + d) % 4) * 8 + z)

    def z_peer(d):
        return (grp, x * 8 + (z + d) % 8)

    partner = (y * 2 + 1 - core, seq)
    peers = [partner] + [y_peer(d) for d in (1, 2, 3)] + [x_peer(d) for d in (1, 2, 3)]
    peers += [z_peer(d) for d in range(1, 8)]
    barrier = pltpu.get_barrier_semaphore()
    for peer in peers:
        pl.semaphore_signal(barrier, inc=1, device_id=peer, device_id_type=MESH)

    count = [0]

    def copy(src, dst, peer):
        i = count[0]
        count[0] += 1
        return pltpu.make_async_remote_copy(
            src_ref=src, dst_ref=dst, send_sem=send.at[i], recv_sem=recv.at[i],
            device_id=peer, device_id_type=MESH,
        )

    def chunk(block, side):
        cols = pl.ds(pl.multiple_of(block * 256 + side * 128, 128), 128)
        parts = [
            mm(ref[:, cols].T, dkv_ref[b * rows : (b + 1) * rows, :])
            for b, ref in enumerate((prev_ref, own_ref, next_ref))
        ]
        return parts[0] + parts[1] + parts[2]

    l_out[0] = loss_ref[...]
    to_core = [copy(core_out.at[i], core_in.at[i], partner) for i in range(4)]
    for i in range(4):
        core_out[i] = chunk((y + 2 + i) % 4, 1 - core).astype(bf16)
        if i == 0:
            pl.semaphore_wait(barrier, len(peers))
            loss_core = copy(l_out.at[0], l_in.at[0], partner)
            loss_core.start()
        to_core[i].start()
    for i in range(4):
        acc[i] = chunk((y + 2 + i) % 4, core)
    loss_core.wait()
    l_out[1] = l_out[0] + l_in[0]
    loss_y = [copy(l_out.at[1], l_in.at[d], y_peer(d)) for d in (1, 2, 3)]
    for c in loss_y:
        c.start()

    to_core[0].wait()
    acc[0] = acc[0] + core_in[0].astype(f32)
    a1 = [copy(a1_out.at[i], a1_in.at[i], y_peer((1, 3)[i])) for i in range(2)]
    for i in range(2):
        a1_out[i] = acc[0, :, i * quarter : (i + 1) * quarter].astype(bf16)
        a1[i].start()
    for i in range(1, 4):
        to_core[i].wait()
        acc[i] = acc[i] + core_in[i].astype(f32)

    def x_rows(d):
        return pl.ds(pl.multiple_of(((x + d) % 4) * 32, 32), 32)

    b1 = [copy(b1_out.at[i], b1_in.at[i], x_peer((1, 3)[i])) for i in range(2)]
    for i in range(2):
        cols = slice(half + i * quarter, half + (i + 1) * quarter)
        b1_out[i] = acc[:, x_rows(2), cols].astype(bf16)
        b1[i].start()

    a2 = [copy(a2_out.at[i], a2_in.at[i], y_peer((1, 3)[i])) for i in range(2)]
    b2 = [copy(b2_out.at[i], b2_in.at[i], x_peer((1, 3)[i])) for i in range(2)]
    for i in range(2):
        lo, hi = slice(i * quarter, (i + 1) * quarter), slice((1 - i) * quarter, (2 - i) * quarter)
        slot = (3, 1)[i]
        a1[i].wait()
        a2_out[i, :, lo] = (acc[slot, :, lo] + a1_in[i].astype(f32)).astype(bf16)
        a2_out[i, :, hi] = acc[slot, :, hi].astype(bf16)
        a2[i].start()
    for i in range(2):
        lo, hi = slice(i * quarter, (i + 1) * quarter), slice((1 - i) * quarter, (2 - i) * quarter)
        mine = slice(half + i * quarter, half + (i + 1) * quarter)
        rest = slice(half + (1 - i) * quarter, half + (2 - i) * quarter)
        d = (1, 3)[i]
        b1[i].wait()
        b2_out[i, :, :, lo] = (acc[:, x_rows(d), mine] + b1_in[i].astype(f32)).astype(bf16)
        b2_out[i, :, :, hi] = acc[:, x_rows(d), rest].astype(bf16)
        b2[i].start()

    for c in loss_y:
        c.wait()
    l_out[2] = l_out[1] + l_in[1] + l_in[2] + l_in[3]
    loss_x = [copy(l_out.at[2], l_in.at[3 + d], x_peer(d)) for d in (1, 2, 3)]
    for c in loss_x:
        c.start()

    a2[0].wait()
    a2[1].wait()
    a_sum[...] = acc[2, :, 0:half] + a2_in[0].astype(f32) + a2_in[1].astype(f32)
    a3 = [copy(a3_out.at[d - 1], a3_in.at[d - 1], x_peer(d)) for d in (1, 2, 3)]
    for d in (1, 2, 3):
        a3_out[d - 1] = a_sum[x_rows(d), :].astype(bf16)
        a3[d - 1].start()
    b2[0].wait()
    b2[1].wait()
    b_sum[...] = acc[:, x_rows(0), half:] + b2_in[0].astype(f32) + b2_in[1].astype(f32)
    b3 = [copy(b3_out.at[d - 1], b3_in.at[d - 1], y_peer(d)) for d in (1, 2, 3)]
    for d in (1, 2, 3):
        b3_out[d - 1] = b_sum[(2 + d) % 4].astype(bf16)
        b3[d - 1].start()

    for c in loss_x:
        c.wait()
    l_out[3] = l_out[2] + l_in[4] + l_in[5] + l_in[6]
    loss_z = [copy(l_out.at[3], l_in.at[6 + d], z_peer(d)) for d in range(1, 8)]
    for c in loss_z:
        c.start()

    for c in a3:
        c.wait()
    a_end = a_sum[x_rows(0), :] + (a3_in[0].astype(f32) + a3_in[1].astype(f32) + a3_in[2].astype(f32))
    for c in b3:
        c.wait()
    b_end = b_sum[2] + (b3_in[0].astype(f32) + b3_in[1].astype(f32) + b3_in[2].astype(f32))
    for i in range(8):
        z_out[i, :, 0:half] = a_end[4 * i : 4 * i + 4]
        z_out[i, :, half:] = b_end[4 * i : 4 * i + 4]
    to_z = [copy(z_out.at[(z + d) % 8], z_in.at[d - 1], z_peer(d)) for d in range(1, 8)]
    for c in to_z:
        c.start()
    for c in loss_z:
        c.wait()
    total = l_out[3]
    for d in range(1, 8):
        total = total + l_in[6 + d]
    total_ref[...] = total
    for c in to_z:
        c.wait()
    grad = z_out[z]
    for d in range(1, 8):
        grad = grad + z_in[d - 1]
    grad_ref[...] = grad


def reduce_grad(prev, own, after, dkv, loss):
    f32, bf16 = jnp.float32, jnp.bfloat16
    width = dkv.shape[1]
    half, quarter = width // 2, width // 4

    def both(*shape):
        return [pltpu.VMEM(shape, bf16), pltpu.VMEM(shape, bf16)]

    return pl.pallas_call(
        reduce_kernel,
        out_shape=(
            jax.ShapeDtypeStruct((4, width), f32),
            jax.ShapeDtypeStruct((8, 128), f32),
        ),
        in_specs=[VMEM] * 5,
        out_specs=(VMEM, VMEM),
        scratch_shapes=[
            pltpu.VMEM((4, 128, width), f32),
            *both(4, 128, width),
            *both(2, 128, quarter),
            *both(2, 4, 32, quarter),
            *both(2, 128, half),
            *both(2, 4, 32, half),
            pltpu.VMEM((128, half), f32),
            pltpu.VMEM((4, 32, half), f32),
            *both(3, 32, half),
            *both(3, 32, half),
            pltpu.VMEM((8, 4, width), f32),
            pltpu.VMEM((7, 4, width), f32),
            pltpu.VMEM((4, 8, 128), f32),
            pltpu.VMEM((14, 8, 128), f32),
            pltpu.SemaphoreType.DMA((39,)),
            pltpu.SemaphoreType.DMA((39,)),
        ],
        compiler_params=pltpu.CompilerParams(
            collective_id=1, has_side_effects=True, vmem_limit_bytes=48 * 2**20
        ),
        name="reduce_grad",
    )(prev, own, after, dkv, loss)


def shifted(array, axis, by):
    peers = lax.axis_size(axis)
    pairs = [(i, i + by) for i in range(peers) if 0 <= i + by < peers]
    return lax.ppermute(array, axis, pairs)


def attend_frames(patch_major, width):
    frame_count, patch_count, _ = patch_major.shape
    head_size = width // HEADS
    queries = patch_major[..., :width].reshape(frame_count, patch_count, HEADS, head_size)
    keys = patch_major[..., width : 2 * width].reshape(frame_count, patch_count, HEADS, head_size)
    values = patch_major[..., 2 * width :].reshape(frame_count, patch_count, HEADS, head_size)
    scores = jnp.einsum(
        "fphd,gphd->phfg", queries, keys, preferred_element_type=jnp.float32
    ) * head_size ** (-0.5)
    probs_b = jax.nn.softmax(scores, axis=-1).astype(jnp.bfloat16)
    result = jnp.einsum("phfg,gphd->fphd", probs_b, values, preferred_element_type=jnp.float32)
    return result.reshape(frame_count, patch_count, width).astype(jnp.bfloat16)


def local(
    video_stream,
    video_qkv,
    out_weight,
    text_states,
    query_weight,
    kv_weight,
    read_weight,
    block_mask,
    pair_labels,
):
    width = out_weight.shape[1]
    shard = jnp.concatenate(
        [query_weight, out_weight, kv_weight[:, :width], kv_weight[:, width:]], axis=0
    )
    weights = lax.all_gather(shard, ("grp", "seq"), axis=0, tiled=False)
    q_rows, o_rows = query_weight.shape[0], out_weight.shape[0]
    wq = weights[:, :q_rows].reshape(-1, width)
    wo = weights[:, q_rows : q_rows + o_rows].reshape(-1, width)
    wk = weights[:, q_rows + o_rows : q_rows + 2 * o_rows].reshape(-1, width)
    wv = weights[:, q_rows + 2 * o_rows :].reshape(-1, width)
    wkv = jnp.concatenate([wk, wv], axis=1)
    patch_major = lax.all_to_all(video_qkv[0], "seq", split_axis=1, concat_axis=0, tiled=True)
    temporal = attend_frames(patch_major, width)
    frame_major = lax.all_to_all(temporal, "seq", split_axis=0, concat_axis=1, tiled=True)
    row_count = frame_major.shape[0] * frame_major.shape[1]
    stream_rows = video_stream[0].reshape(row_count, width)
    mixed = (
        stream_rows.astype(jnp.float32)
        + mm(frame_major.reshape(row_count, width), wo)
    ).astype(jnp.bfloat16)
    queries = mm(text_states[0], wq).astype(jnp.bfloat16) * jnp.bfloat16(0.125)
    prev = shifted(mixed, "seq", 1)
    after = shifted(mixed, "seq", -1)
    pair_count = lax.axis_size("grp") * lax.axis_size("seq")
    read = jnp.broadcast_to(read_weight[:, None], (width, 128))
    reward, loss_value, d_kv = cross(
        block_mask[0, 0], pair_labels[0], queries, prev, mixed, after, wkv, read, pair_count
    )
    kv_grad, total = reduce_grad(prev, mixed, after, d_kv, loss_value)
    return (reward[0:1, 0:1], total[0, 0] / pair_count, kv_grad)


def solution(mesh):
    placed = (
        P("grp", "seq", None, None),
        P("grp", "seq", None, None),
        P(("grp", "seq"), None),
        P("grp", "seq", None),
        P(("grp", "seq"), None),
        P(("grp", "seq"), None),
        P(),
        P("grp", "seq", None),
        P("grp", "seq"),
    )
    return jax.shard_map(
        local,
        mesh=mesh,
        in_specs=placed,
        out_specs=(P("grp", "seq"), P(), P(("grp", "seq"), None)),
        check_vma=False,
    )
```

```python
import functools
import jax
import jax.numpy as jnp
from jax import lax
from jax.experimental import pallas as pl
from jax.experimental.pallas import tpu as pltpu
from jax.sharding import PartitionSpec as P

HEADS = 16
MESH = pl.DeviceIdType.MESH
EPSILON = 1e-06
NN = (((1,), (0,)), ((), ()))
NT = (((1,), (1,)), ((), ()))
VMEM = pl.BlockSpec(memory_space=pltpu.VMEM)
SMEM = pl.BlockSpec(memory_space=pltpu.SMEM)


def mm(a, b, dims=NN):
    return lax.dot_general(a, b, dims, preferred_element_type=jnp.float32)


def cross_kernel(
    pair_count, mask_ref, label_ref, q_ref, kv, read_ref,
    reward_ref, loss_ref, dkv_ref, vt, exps, inverse, out_t, slopes, d_out_t, d_out,
):
    tokens, width = q_ref.shape
    rows = kv.shape[0] // 3
    pairs = width // 128
    blocks = [pl.ds(b * rows, rows) for b in range(3)]

    lane = lax.broadcasted_iota(jnp.int32, (1, 128), 1)
    sides = [((lane // 64) == h).astype(jnp.bfloat16) for h in range(2)]
    bias = [jnp.where(mask_ref[b] == 1, 0.0, -jnp.inf).astype(jnp.float32) for b in range(3)]

    def forward(j, squares):
        cols = pl.ds(pl.multiple_of(j * 128, 128), 128)
        vcols = pl.ds(pl.multiple_of(width + j * 128, 128), 128)
        vt[cols, :] = kv[:, vcols].T
        k = kv[:, cols]
        q = q_ref[:, cols]
        for h in range(2):
            s = mm(k, q * sides[h], NT)
            s = [s[b * rows : (b + 1) * rows] for b in range(3)]
            top = [jnp.max(s[b], axis=0, keepdims=True) + bias[b] for b in range(3)]
            top = jnp.maximum(jnp.maximum(top[0], top[1]), top[2])
            total = jnp.zeros((1, tokens), jnp.float32)
            for b in range(3):
                e = jnp.exp(s[b] - (top - bias[b]))
                exps[2 * j + h, blocks[b], :] = e
                total = total + jnp.sum(e, axis=0, keepdims=True)
            inv = 1.0 / total
            inverse[2 * j + h] = jnp.broadcast_to(inv, (8, tokens))
            p = (exps[2 * j + h] * inv).astype(jnp.bfloat16)
            mine = pl.ds(pl.multiple_of(j * 128 + h * 64, 64), 64)
            o = mm(vt[mine, :], p)
            out_t[mine, :] = o
            squares = squares + jnp.sum(o * o, axis=0, keepdims=True)
        return squares

    squares = lax.fori_loop(0, pairs, forward, jnp.zeros((1, tokens), jnp.float32))
    inv_root = 1.0 / jnp.sqrt(squares / width + EPSILON)

    def rewards(j, carry):
        reward, inner = carry
        cols = pl.ds(pl.multiple_of(j * 128, 128), 128)
        normed = out_t[cols, :] * inv_root
        gates = jax.nn.sigmoid(normed)
        read = read_ref[cols, 0:1]
        scaled = read * gates
        slope = scaled * (1.0 + normed * (1.0 - gates))
        slopes[cols, :] = slope
        reward = reward + jnp.sum(scaled * normed, axis=0, keepdims=True)
        inner = inner + jnp.sum(slope * normed, axis=0, keepdims=True)
        return reward, inner

    zero = jnp.zeros((1, tokens), jnp.float32)
    reward, inner = lax.fori_loop(0, pairs, rewards, (zero, zero))
    reward = jnp.sum(reward, axis=1, keepdims=True) / tokens
    signed = 2.0 * label_ref[0].astype(jnp.float32) - 1.0
    x = -signed * reward
    loss = jnp.maximum(x, 0.0) + jnp.log1p(jnp.exp(-jnp.abs(x)))
    reward_ref[...] = jnp.broadcast_to(reward, reward_ref.shape)
    loss_ref[...] = jnp.broadcast_to(loss, loss_ref.shape)
    factor = -signed * jax.nn.sigmoid(x) / pair_count / tokens
    inner = inner / width

    @pl.loop(0, pairs)
    def _(j):
        cols = pl.ds(pl.multiple_of(j * 128, 128), 128)
        normed = out_t[cols, :] * inv_root
        d = ((slopes[cols, :] - normed * inner) * (inv_root * factor)).astype(jnp.bfloat16)
        d_out_t[cols, :] = d
        d_out[:, cols] = d.T

    @pl.loop(0, pairs)
    def _(j):
        cols = pl.ds(pl.multiple_of(j * 128, 128), 128)
        vcols = pl.ds(pl.multiple_of(width + j * 128, 128), 128)
        v = kv[:, vcols]
        q = q_ref[:, cols]
        do = d_out[:, cols]
        empty = jnp.zeros((64, tokens), jnp.bfloat16)
        dk = dv = None
        for h in range(2):
            mine = d_out_t[pl.ds(pl.multiple_of(j * 128 + h * 64, 64), 64), :]
            mine = jnp.concatenate([mine, empty] if h == 0 else [empty, mine], axis=0)
            dp = mm(v, mine)
            p = exps[2 * j + h] * inverse[2 * j + h, 0:1, :]
            both = p * dp
            ds = (both - p * jnp.sum(both, axis=0, keepdims=True)).astype(jnp.bfloat16)
            dkh = mm(ds, q * sides[h])
            dvh = mm(p.astype(jnp.bfloat16), do * sides[h])
            dk = dkh if dk is None else dk + dkh
            dv = dvh if dv is None else dv + dvh
        dkv_ref[:, cols] = dk.astype(jnp.bfloat16)
        dkv_ref[:, vcols] = dv.astype(jnp.bfloat16)


def cross(mask, label, q, kv, read, pair_count):
    tokens, width = q.shape
    keys = kv.shape[0]
    f32, bf16 = jnp.float32, jnp.bfloat16
    return pl.pallas_call(
        functools.partial(cross_kernel, pair_count),
        out_shape=(
            jax.ShapeDtypeStruct((8, 128), f32),
            jax.ShapeDtypeStruct((8, 128), f32),
            jax.ShapeDtypeStruct((keys, 2 * width), bf16),
        ),
        in_specs=[SMEM, SMEM] + [VMEM] * 3,
        out_specs=(VMEM, VMEM, VMEM),
        scratch_shapes=[
            pltpu.VMEM((width, keys), bf16),
            pltpu.VMEM((HEADS, keys, tokens), f32),
            pltpu.VMEM((HEADS, 8, tokens), f32),
            pltpu.VMEM((width, tokens), f32),
            pltpu.VMEM((width, tokens), f32),
            pltpu.VMEM((width, tokens), bf16),
            pltpu.VMEM((tokens, width), bf16),
        ],
        compiler_params=pltpu.CompilerParams(vmem_limit_bytes=60 * 2**20),
        name="cross",
    )(mask, label, q, kv, read)


def prepare_kernel(
    qkv_ref, shard_ref, text_ref, stream_ref, q_ref, ctx_ref, kv_ref,
    stage, got, mixed_out, frame, back, text, stream, shards, q_tmp, s_tmp, wq, small, halo,
    local_sem, z_send, z_recv, go_send, go_recv, ret_send, ret_recv, w_send, w_recv, h_send, h_recv,
):
    f32, bf16 = jnp.float32, jnp.bfloat16
    grp, seq = lax.axis_index("grp"), lax.axis_index("seq")
    y, core = grp // 2, grp % 2
    x, z = seq // 8, seq % 8
    width = wq.shape[1]
    rows = frame.shape[0]

    def seq_at(d):
        return ((x + d // 8) % 4) * 8 + (z + d % 8) % 8

    def y_peer(d):
        return (((y + d) % 4) * 2 + core, seq)

    def x_peer(d):
        return (grp, ((x + d) % 4) * 8 + z)

    partner = (y * 2 + 1 - core, seq)
    barrier = pltpu.get_barrier_semaphore()

    locals_ = []
    for part in range(3):
        for side in range(2):
            start = part * width + side * (width // 2)
            locals_.append(pltpu.make_async_copy(
                qkv_ref.at[:, :, start : start + width // 2], stage.at[:, side, part],
                local_sem.at[part * 2 + side],
            ))
    load_text = pltpu.make_async_copy(text_ref, text, local_sem.at[6])
    load_stream = pltpu.make_async_copy(stream_ref, stream, local_sem.at[7])
    for c in locals_ + [load_text, load_stream]:
        c.start()

    @pl.loop(1, 32)
    def _(d):
        pl.semaphore_signal(barrier, inc=1, device_id=(grp, seq_at(d)), device_id_type=MESH)

    for peer in (partner, y_peer(1), y_peer(3)):
        pl.semaphore_signal(barrier, inc=1, device_id=peer, device_id_type=MESH)
    shards[z] = shard_ref[...]
    pl.semaphore_wait(barrier, 34)

    def remote(src, dst, sems, i, peer):
        return pltpu.make_async_remote_copy(
            src_ref=src, dst_ref=dst, send_sem=sems[0].at[i], recv_sem=sems[1].at[i],
            device_id=peer, device_id_type=MESH,
        )

    def z_copy(d):
        return remote(shard_ref, shards.at[z], (z_send, z_recv), d, (grp, x * 8 + (z + d) % 8))

    def go(d):
        t = seq_at(d)
        return remote(stage.at[t // 2, t % 2], got.at[seq], (go_send, go_recv), d, (grp, t))

    def ret(d):
        t = seq_at(d)
        where = (pl.ds(pl.multiple_of(seq // 2 * 16, 16), 16), pl.ds(pl.multiple_of(seq % 2 * (width // 2), 128), width // 2))
        return remote(back.at[t], frame.at[where], (ret_send, ret_recv), d, (grp, t))

    for d in (1, 7, 2, 6, 3, 5, 4):
        z_copy(d).start()
    for c in locals_:
        c.wait()

    @pl.loop(1, 32)
    def _(d):
        go(d).start()

    got[seq] = stage[seq // 2, seq % 2]

    for d in range(1, 8):
        z_copy(d).wait()
    for i in range(8):
        w = shards[i].astype(f32)
        q_tmp[14 * i : 14 * i + 14, :] = w[0:14]
        for k in range(3):
            s_tmp[4 * i : 4 * i + 4, k * width : (k + 1) * width] = w[16 + 4 * k : 20 + 4 * k]

    counter = [0]

    def block(unit, yy, xx, lo, n):
        first = (((y + yy) % 4) * 8 + core * 4 + (x + xx) % 4) * unit + lo
        return pl.ds(pl.multiple_of(first, 16), n)

    def spread(ref, unit, cut, first, second, flip):
        at = (lambda a, b, lo, n: block(unit, b, a, lo, n)) if flip else (lambda a, b, lo, n: block(unit, a, b, lo, n))

        def send(a, b, lo, n, peer):
            i = counter[0]
            counter[0] += 1
            span = at(a, b, lo, n)
            c = remote(ref.at[span, :], ref.at[span, :], (w_send, w_recv), i, peer)
            c.start()
            return c

        started = []

        def out(peer_of, a, b):
            pair = [send(a, b, 0, unit, peer_of(1)), send(a, b, 0, unit, peer_of(3))]
            started.extend(pair)
            return pair

        def on(peer_of, a, b, along_first):
            if along_first:
                pair = [send(a - 1, b, 0, cut, peer_of(1)), send(a + 1, b, cut, unit - cut, peer_of(3))]
            else:
                pair = [send(a, b - 1, 0, cut, peer_of(1)), send(a, b + 1, cut, unit - cut, peer_of(3))]
            started.extend(pair)
            return pair

        def arrived(pair):
            for c in pair:
                c.wait_recv()

        state = {}

        def step0():
            state["f"] = out(first, 0, 0)
            state[0] = out(second, 0, 0)

        def step1():
            arrived(state["f"])
            state["ff"] = on(first, 0, 0, True)
            state[3] = out(second, 3, 0)
            state[1] = out(second, 1, 0)

        def step2():
            arrived(state["ff"])
            state[2] = out(second, 2, 0)

        def forward(a):
            arrived(state[a])
            state["s", a] = on(second, a, 0, False)

        def finish():
            for a in range(4):
                arrived(state["s", a])

        return started, step0, step1, step2, forward, finish

    q_sent, q0, q1, q2, q_on, q_end = spread(wq, 112, 64, x_peer, y_peer, True)
    s_sent, s0, s1, s2, s_on, s_end = spread(small, 32, 16, y_peer, x_peer, False)

    wq[block(112, 0, 0, 0, 112), :] = q_tmp[...].astype(bf16)
    q0()
    small[block(32, 0, 0, 0, 32), :] = s_tmp[...].astype(bf16)
    s0()
    q1()
    s1()
    q2()
    s2()
    for a in (0, 3, 1):
        q_on(a)
        s_on(a)

    @pl.loop(1, 32)
    def _(d):
        go(d).wait_recv()

    count = 32 * 16
    lane = lax.broadcasted_iota(jnp.int32, (1, 128), 1)
    sides = [((lane // 64) == h).astype(bf16) for h in range(2)]

    def temporal(j):
        cols = slice(j * 128, j * 128 + 128)
        q = got[:, 0, :, cols].reshape(count, 128)
        k = got[:, 1, :, cols].reshape(count, 128)
        v = got[:, 2, :, cols].reshape(count, 128)
        other = (
            lax.broadcasted_iota(jnp.int32, (count, count), 0) % 16
            != lax.broadcasted_iota(jnp.int32, (count, count), 1) % 16
        )
        total = None
        for h in range(2):
            s = mm(q * (sides[h] * jnp.asarray(0.125, bf16)), k, NT)
            s = jnp.where(other, -jnp.inf, s)
            e = jnp.exp(s - jnp.max(s, axis=1, keepdims=True))
            p = (e * (1.0 / jnp.sum(e, axis=1, keepdims=True))).astype(bf16)
            o = mm(p, v * sides[h])
            total = o if total is None else total + o
        back[:, :, cols] = total.astype(bf16).reshape(32, 16, 128)

    for j in range(4):
        temporal(j)

    @pl.loop(1, 32)
    def _(d):
        ret(d).start()

    mine = (pl.ds(pl.multiple_of(seq // 2 * 16, 16), 16), pl.ds(pl.multiple_of(seq % 2 * (width // 2), 128), width // 2))
    frame[mine] = back[seq]

    q_on(2)
    s_on(2)

    def to_partner(ref, unit, yy):
        i = counter[0]
        counter[0] += 1
        span = pl.ds(pl.multiple_of((((y + yy) % 4) * 2 + core) * 4 * unit, 16), 4 * unit)
        c = remote(ref.at[span, :], ref.at[span, :], (w_send, w_recv), i, partner)
        c.start()
        return c

    q_core = [to_partner(wq, 112, yy) for yy in (0, 3, 1)]
    s_end()
    s_core = [to_partner(small, 32, yy) for yy in (0, 3, 1, 2)]
    q_end()
    q_core.append(to_partner(wq, 112, 2))

    @pl.loop(1, 32)
    def _(d):
        ret(d).wait_recv()

    for c in s_core:
        c.wait_recv()
    load_stream.wait()

    halos = []
    part = 64
    for i in range(rows // part):
        span = slice(i * part, (i + 1) * part)
        mixed = (stream[span, :].astype(f32) + mm(frame[span, :], small[:, 0:width])).astype(bf16)
        mixed_out[span, :] = mixed
        for s, d in ((0, 1), (1, 31)):
            c = remote(
                mixed_out.at[span, :], halo.at[s, span, :], (h_send, h_recv), 2 * i + s,
                (grp, (seq + d) % 32),
            )
            c.start()
            halos.append(c)

    def keys_values(b, m):
        for c in range(4):
            cols = slice(c * (width // 2), (c + 1) * (width // 2))
            kv_ref[b * rows : (b + 1) * rows, cols] = mm(m, small[:, width + c * (width // 2) : width + (c + 1) * (width // 2)]).astype(bf16)

    ctx_ref[rows : 2 * rows, :] = mixed_out[...]
    keys_values(1, mixed_out[...])
    for c in q_core:
        c.wait_recv()
    load_text.wait()
    tokens = text.shape[0]
    for i in range(2):
        span = slice(i * (tokens // 2), (i + 1) * (tokens // 2))
        for k in range(2):
            cols = slice(k * (width // 2), (k + 1) * (width // 2))
            q_ref[span, cols] = (mm(text[span, :], wq[:, cols]).astype(bf16) * jnp.asarray(0.125, bf16))
    for c in halos:
        c.wait_recv()
    for s, b in ((0, 0), (1, 2)):
        ctx_ref[b * rows : (b + 1) * rows, :] = halo[s]
        keys_values(b, halo[s])

    for c in halos + q_sent + s_sent + q_core + s_core:
        c.wait_send()

    @pl.loop(1, 32)
    def _(d):
        go(d).wait_send()
        ret(d).wait_send()


def prepare(qkv, shard, text, stream):
    f32, bf16 = jnp.float32, jnp.bfloat16
    tokens, depth = text.shape
    rows, width = stream.shape
    any_ = pl.BlockSpec(memory_space=pl.ANY)
    dma = pltpu.SemaphoreType.DMA
    return pl.pallas_call(
        prepare_kernel,
        out_shape=(
            jax.ShapeDtypeStruct((tokens, width), bf16),
            jax.ShapeDtypeStruct((3 * rows, width), bf16),
            jax.ShapeDtypeStruct((3 * rows, 2 * width), bf16),
        ),
        in_specs=[any_, VMEM, any_, any_],
        out_specs=(VMEM, VMEM, VMEM),
        scratch_shapes=[
            pltpu.VMEM((16, 2, 3, 16, width // 2), bf16),
            pltpu.VMEM((32, 3, 16, width // 2), bf16),
            pltpu.VMEM((rows, width), bf16),
            pltpu.VMEM((rows, width), bf16),
            pltpu.VMEM((32, 16, width // 2), bf16),
            pltpu.VMEM((tokens, depth), bf16),
            pltpu.VMEM((rows, width), bf16),
            pltpu.VMEM((8, 32, width), bf16),
            pltpu.VMEM((112, width), f32),
            pltpu.VMEM((32, 3 * width), f32),
            pltpu.VMEM((depth, width), bf16),
            pltpu.VMEM((width, 3 * width), bf16),
            pltpu.VMEM((2, rows, width), bf16),
            dma((8,)), dma((8,)), dma((8,)), dma((32,)), dma((32,)), dma((32,)), dma((32,)),
            dma((64,)), dma((64,)), dma((8,)), dma((8,)),
        ],
        compiler_params=pltpu.CompilerParams(
            collective_id=2, has_side_effects=True, vmem_limit_bytes=56 * 2**20
        ),
        name="prepare",
    )(qkv, shard, text, stream)


def reduce_kernel(
    ctx_ref, dkv_ref, loss_ref, grad_ref, total_ref,
    acc, core_out, core_in, a1_out, a1_in, b1_out, b1_in, a2_out, a2_in, b2_out, b2_in,
    a_sum, b_sum, a3_out, a3_in, b3_out, b3_in, z_out, z_in, l_out, l_in, send, recv,
):
    f32, bf16 = jnp.float32, jnp.bfloat16
    grp, seq = lax.axis_index("grp"), lax.axis_index("seq")
    y, core = grp // 2, grp % 2
    x, z = seq // 8, seq % 8
    rows = ctx_ref.shape[0] // 3
    half = acc.shape[2] // 2
    quarter = half // 2

    def y_peer(d):
        return (((y + d) % 4) * 2 + core, seq)

    def x_peer(d):
        return (grp, ((x + d) % 4) * 8 + z)

    def z_peer(d):
        return (grp, x * 8 + (z + d) % 8)

    partner = (y * 2 + 1 - core, seq)
    peers = [partner] + [y_peer(d) for d in (1, 2, 3)] + [x_peer(d) for d in (1, 2, 3)]
    peers += [z_peer(d) for d in range(1, 8)]
    barrier = pltpu.get_barrier_semaphore()
    for peer in peers:
        pl.semaphore_signal(barrier, inc=1, device_id=peer, device_id_type=MESH)

    count = [0]

    def copy(src, dst, peer):
        i = count[0]
        count[0] += 1
        return pltpu.make_async_remote_copy(
            src_ref=src, dst_ref=dst, send_sem=send.at[i], recv_sem=recv.at[i],
            device_id=peer, device_id_type=MESH,
        )

    def chunk(block, side):
        cols = pl.ds(pl.multiple_of(block * 256 + side * 128, 128), 128)
        parts = [
            mm(ctx_ref[b * rows : (b + 1) * rows, cols].T, dkv_ref[b * rows : (b + 1) * rows, :])
            for b in range(3)
        ]
        return parts[0] + parts[1] + parts[2]

    l_out[0] = loss_ref[...]
    to_core = [copy(core_out.at[i], core_in.at[i], partner) for i in range(4)]
    for i in range(4):
        core_out[i] = chunk((y + 2 + i) % 4, 1 - core).astype(bf16)
        if i == 0:
            pl.semaphore_wait(barrier, len(peers))
            loss_core = copy(l_out.at[0], l_in.at[0], partner)
            loss_core.start()
        to_core[i].start()
    for i in range(4):
        acc[i] = chunk((y + 2 + i) % 4, core)
    loss_core.wait()
    l_out[1] = l_out[0] + l_in[0]
    loss_y = [copy(l_out.at[1], l_in.at[d], y_peer(d)) for d in (1, 2, 3)]
    for c in loss_y:
        c.start()

    to_core[0].wait()
    acc[0] = acc[0] + core_in[0].astype(f32)
    a1 = [copy(a1_out.at[i], a1_in.at[i], y_peer((1, 3)[i])) for i in range(2)]
    for i in range(2):
        a1_out[i] = acc[0, :, i * quarter : (i + 1) * quarter].astype(bf16)
        a1[i].start()
    for i in range(1, 4):
        to_core[i].wait()
        acc[i] = acc[i] + core_in[i].astype(f32)

    def x_rows(d):
        return pl.ds(pl.multiple_of(((x + d) % 4) * 32, 32), 32)

    b1 = [copy(b1_out.at[i], b1_in.at[i], x_peer((1, 3)[i])) for i in range(2)]
    for i in range(2):
        cols = slice(half + i * quarter, half + (i + 1) * quarter)
        b1_out[i] = acc[:, x_rows(2), cols].astype(bf16)
        b1[i].start()

    a2 = [copy(a2_out.at[i], a2_in.at[i], y_peer((1, 3)[i])) for i in range(2)]
    b2 = [copy(b2_out.at[i], b2_in.at[i], x_peer((1, 3)[i])) for i in range(2)]
    for i in range(2):
        lo, hi = slice(i * quarter, (i + 1) * quarter), slice((1 - i) * quarter, (2 - i) * quarter)
        slot = (3, 1)[i]
        a1[i].wait()
        a2_out[i, :, lo] = (acc[slot, :, lo] + a1_in[i].astype(f32)).astype(bf16)
        a2_out[i, :, hi] = acc[slot, :, hi].astype(bf16)
        a2[i].start()
    for i in range(2):
        lo, hi = slice(i * quarter, (i + 1) * quarter), slice((1 - i) * quarter, (2 - i) * quarter)
        mine = slice(half + i * quarter, half + (i + 1) * quarter)
        rest = slice(half + (1 - i) * quarter, half + (2 - i) * quarter)
        d = (1, 3)[i]
        b1[i].wait()
        b2_out[i, :, :, lo] = (acc[:, x_rows(d), mine] + b1_in[i].astype(f32)).astype(bf16)
        b2_out[i, :, :, hi] = acc[:, x_rows(d), rest].astype(bf16)
        b2[i].start()

    for c in loss_y:
        c.wait()
    l_out[2] = l_out[1] + l_in[1] + l_in[2] + l_in[3]
    loss_x = [copy(l_out.at[2], l_in.at[3 + d], x_peer(d)) for d in (1, 2, 3)]
    for c in loss_x:
        c.start()

    a2[0].wait()
    a2[1].wait()
    a_sum[...] = acc[2, :, 0:half] + a2_in[0].astype(f32) + a2_in[1].astype(f32)
    a3 = [copy(a3_out.at[d - 1], a3_in.at[d - 1], x_peer(d)) for d in (1, 2, 3)]
    for d in (1, 2, 3):
        a3_out[d - 1] = a_sum[x_rows(d), :].astype(bf16)
        a3[d - 1].start()
    b2[0].wait()
    b2[1].wait()
    b_sum[...] = acc[:, x_rows(0), half:] + b2_in[0].astype(f32) + b2_in[1].astype(f32)
    b3 = [copy(b3_out.at[d - 1], b3_in.at[d - 1], y_peer(d)) for d in (1, 2, 3)]
    for d in (1, 2, 3):
        b3_out[d - 1] = b_sum[(2 + d) % 4].astype(bf16)
        b3[d - 1].start()

    for c in loss_x:
        c.wait()
    l_out[3] = l_out[2] + l_in[4] + l_in[5] + l_in[6]
    loss_z = [copy(l_out.at[3], l_in.at[6 + d], z_peer(d)) for d in range(1, 8)]
    for c in loss_z:
        c.start()

    for c in a3:
        c.wait()
    a_end = a_sum[x_rows(0), :] + (a3_in[0].astype(f32) + a3_in[1].astype(f32) + a3_in[2].astype(f32))
    for c in b3:
        c.wait()
    b_end = b_sum[2] + (b3_in[0].astype(f32) + b3_in[1].astype(f32) + b3_in[2].astype(f32))
    for i in range(8):
        z_out[i, :, 0:half] = a_end[4 * i : 4 * i + 4]
        z_out[i, :, half:] = b_end[4 * i : 4 * i + 4]
    to_z = [copy(z_out.at[(z + d) % 8], z_in.at[d - 1], z_peer(d)) for d in range(1, 8)]
    for c in to_z:
        c.start()
    for c in loss_z:
        c.wait()
    total = l_out[3]
    for d in range(1, 8):
        total = total + l_in[6 + d]
    total_ref[...] = total
    for c in to_z:
        c.wait()
    grad = z_out[z]
    for d in range(1, 8):
        grad = grad + z_in[d - 1]
    grad_ref[...] = grad


def reduce_grad(ctx, dkv, loss):
    f32, bf16 = jnp.float32, jnp.bfloat16
    width = dkv.shape[1]
    half, quarter = width // 2, width // 4

    def both(*shape):
        return [pltpu.VMEM(shape, bf16), pltpu.VMEM(shape, bf16)]

    return pl.pallas_call(
        reduce_kernel,
        out_shape=(
            jax.ShapeDtypeStruct((4, width), f32),
            jax.ShapeDtypeStruct((8, 128), f32),
        ),
        in_specs=[VMEM] * 3,
        out_specs=(VMEM, VMEM),
        scratch_shapes=[
            pltpu.VMEM((4, 128, width), f32),
            *both(4, 128, width),
            *both(2, 128, quarter),
            *both(2, 4, 32, quarter),
            *both(2, 128, half),
            *both(2, 4, 32, half),
            pltpu.VMEM((128, half), f32),
            pltpu.VMEM((4, 32, half), f32),
            *both(3, 32, half),
            *both(3, 32, half),
            pltpu.VMEM((8, 4, width), f32),
            pltpu.VMEM((7, 4, width), f32),
            pltpu.VMEM((4, 8, 128), f32),
            pltpu.VMEM((14, 8, 128), f32),
            pltpu.SemaphoreType.DMA((39,)),
            pltpu.SemaphoreType.DMA((39,)),
        ],
        compiler_params=pltpu.CompilerParams(
            collective_id=1, has_side_effects=True, vmem_limit_bytes=48 * 2**20
        ),
        name="reduce_grad",
    )(ctx, dkv, loss)


def local(
    video_stream,
    video_qkv,
    out_weight,
    text_states,
    query_weight,
    kv_weight,
    read_weight,
    block_mask,
    pair_labels,
):
    width = out_weight.shape[1]
    rows = video_stream.shape[2]
    shard = jnp.concatenate(
        [
            jnp.pad(query_weight, ((0, 2), (0, 0))),
            out_weight,
            kv_weight[:, :width],
            kv_weight[:, width:],
            jnp.zeros((4, width), jnp.bfloat16),
        ],
        axis=0,
    )
    qkv = video_qkv.reshape(rows // 16, 16, 3 * width)
    queries, context, keys_values = prepare(
        qkv, shard, text_states[0], video_stream.reshape(rows, width)
    )
    pair_count = lax.axis_size("grp") * lax.axis_size("seq")
    read = jnp.broadcast_to(read_weight[:, None], (width, 128))
    reward, loss_value, d_kv = cross(
        block_mask[0, 0], pair_labels[0], queries, keys_values, read, pair_count
    )
    kv_grad, total = reduce_grad(context, d_kv, loss_value)
    return (reward[0:1, 0:1], total[0, 0] / pair_count, kv_grad)


def solution(mesh):
    placed = (
        P("grp", "seq", None, None),
        P("grp", "seq", None, None),
        P(("grp", "seq"), None),
        P("grp", "seq", None),
        P(("grp", "seq"), None),
        P(("grp", "seq"), None),
        P(),
        P("grp", "seq", None),
        P("grp", "seq"),
    )
    return jax.shard_map(
        local,
        mesh=mesh,
        in_specs=placed,
        out_specs=(P("grp", "seq"), P(), P(("grp", "seq"), None)),
        check_vma=False,
    )
```

```python
import functools
import jax
import jax.numpy as jnp
from jax import lax
from jax.experimental import pallas as pl
from jax.experimental.pallas import tpu as pltpu
from jax.sharding import PartitionSpec as P

HEADS = 16
MESH = pl.DeviceIdType.MESH
EPSILON = 1e-06
NN = (((1,), (0,)), ((), ()))
NT = (((1,), (1,)), ((), ()))
VMEM = pl.BlockSpec(memory_space=pltpu.VMEM)
SMEM = pl.BlockSpec(memory_space=pltpu.SMEM)


def mm(a, b, dims=NN):
    return lax.dot_general(a, b, dims, preferred_element_type=jnp.float32)


def prepare_kernel(
    qkv_ref, wq_ref, wo_ref, wkv_ref, text_ref, stream_ref, q_ref, ctx_ref, kv_ref,
    shard, stage, got, mixed_out, frame, back, text, stream, shards, q_tmp, s_tmp, wq, small, halo,
    local_sem, z_send, z_recv, go_send, go_recv, ret_send, ret_recv, w_send, w_recv, h_send, h_recv,
):
    f32, bf16 = jnp.float32, jnp.bfloat16
    grp, seq = lax.axis_index("grp"), lax.axis_index("seq")
    y, core = grp // 2, grp % 2
    x, z = seq // 8, seq % 8
    width = wq.shape[1]
    rows = frame.shape[0]

    def seq_at(d):
        return ((x + d // 8) % 4) * 8 + (z + d % 8) % 8

    def y_peer(d):
        return (((y + d) % 4) * 2 + core, seq)

    def x_peer(d):
        return (grp, ((x + d) % 4) * 8 + z)

    partner = (y * 2 + 1 - core, seq)
    barrier = pltpu.get_barrier_semaphore()

    locals_ = []
    for part in range(3):
        for side in range(2):
            start = part * width + side * (width // 2)
            locals_.append(pltpu.make_async_copy(
                qkv_ref.at[:, :, start : start + width // 2], stage.at[:, side, part],
                local_sem.at[part * 2 + side],
            ))
    load_text = pltpu.make_async_copy(text_ref, text, local_sem.at[6])
    load_stream = pltpu.make_async_copy(stream_ref, stream, local_sem.at[7])
    for c in locals_ + [load_text, load_stream]:
        c.start()

    @pl.loop(1, 32)
    def _(d):
        pl.semaphore_signal(barrier, inc=1, device_id=(grp, seq_at(d)), device_id_type=MESH)

    for peer in (partner, y_peer(1), y_peer(3)):
        pl.semaphore_signal(barrier, inc=1, device_id=peer, device_id_type=MESH)
    q_tmp[0:14, :] = wq_ref[...].astype(f32)
    q_tmp[16:20, :] = wo_ref[...].astype(f32)
    q_tmp[20:24, :] = wkv_ref[:, 0:width].astype(f32)
    q_tmp[24:28, :] = wkv_ref[:, width:].astype(f32)
    own = q_tmp[0:32, :].astype(bf16)
    shard[...] = own
    shards[z] = own
    pl.semaphore_wait(barrier, 34)

    def remote(src, dst, sems, i, peer):
        return pltpu.make_async_remote_copy(
            src_ref=src, dst_ref=dst, send_sem=sems[0].at[i], recv_sem=sems[1].at[i],
            device_id=peer, device_id_type=MESH,
        )

    def z_copy(d):
        return remote(shard, shards.at[z], (z_send, z_recv), d, (grp, x * 8 + (z + d) % 8))

    def go(d):
        t = seq_at(d)
        return remote(stage.at[t // 2, t % 2], got.at[seq], (go_send, go_recv), d, (grp, t))

    def ret(d):
        t = seq_at(d)
        where = (pl.ds(pl.multiple_of(seq // 2 * 16, 16), 16), pl.ds(pl.multiple_of(seq % 2 * (width // 2), 128), width // 2))
        return remote(back.at[t], frame.at[where], (ret_send, ret_recv), d, (grp, t))

    for d in (1, 7, 2, 6, 3, 5, 4):
        z_copy(d).start()
    for c in locals_:
        c.wait()

    @pl.loop(1, 32)
    def _(d):
        go(d).start()

    got[seq] = stage[seq // 2, seq % 2]

    for d in range(1, 8):
        z_copy(d).wait()
    for i in range(8):
        w = shards[i].astype(f32)
        q_tmp[14 * i : 14 * i + 14, :] = w[0:14]
        for k in range(3):
            s_tmp[4 * i : 4 * i + 4, k * width : (k + 1) * width] = w[16 + 4 * k : 20 + 4 * k]

    counter = [0]

    def block(unit, yy, xx, lo, n):
        first = (((y + yy) % 4) * 8 + core * 4 + (x + xx) % 4) * unit + lo
        return pl.ds(pl.multiple_of(first, 16), n)

    def spread(ref, unit, cut, first, second, flip):
        at = (lambda a, b, lo, n: block(unit, b, a, lo, n)) if flip else (lambda a, b, lo, n: block(unit, a, b, lo, n))

        def send(a, b, lo, n, peer):
            i = counter[0]
            counter[0] += 1
            span = at(a, b, lo, n)
            c = remote(ref.at[span, :], ref.at[span, :], (w_send, w_recv), i, peer)
            c.start()
            return c

        started = []

        def out(peer_of, a, b):
            pair = [send(a, b, 0, unit, peer_of(1)), send(a, b, 0, unit, peer_of(3))]
            started.extend(pair)
            return pair

        def on(peer_of, a, b, along_first):
            if along_first:
                pair = [send(a - 1, b, 0, cut, peer_of(1)), send(a + 1, b, cut, unit - cut, peer_of(3))]
            else:
                pair = [send(a, b - 1, 0, cut, peer_of(1)), send(a, b + 1, cut, unit - cut, peer_of(3))]
            started.extend(pair)
            return pair

        def arrived(pair):
            for c in pair:
                c.wait_recv()

        state = {}

        def step0():
            state["f"] = out(first, 0, 0)
            state[0] = out(second, 0, 0)

        def step1():
            arrived(state["f"])
            state["ff"] = on(first, 0, 0, True)
            state[3] = out(second, 3, 0)
            state[1] = out(second, 1, 0)

        def step2():
            arrived(state["ff"])
            state[2] = out(second, 2, 0)

        def forward(a):
            arrived(state[a])
            state["s", a] = on(second, a, 0, False)

        def finish():
            for a in range(4):
                arrived(state["s", a])

        return started, step0, step1, step2, forward, finish

    q_sent, q0, q1, q2, q_on, q_end = spread(wq, 112, 64, x_peer, y_peer, True)
    s_sent, s0, s1, s2, s_on, s_end = spread(small, 32, 16, y_peer, x_peer, False)

    wq[block(112, 0, 0, 0, 112), :] = q_tmp[...].astype(bf16)
    q0()
    small[block(32, 0, 0, 0, 32), :] = s_tmp[...].astype(bf16)
    s0()
    q1()
    s1()
    q2()
    s2()
    for a in (0, 3, 1):
        q_on(a)
        s_on(a)

    @pl.loop(1, 32)
    def _(d):
        go(d).wait_recv()

    count = 32 * 16
    lane = lax.broadcasted_iota(jnp.int32, (1, 128), 1)
    sides = [((lane // 64) == h).astype(bf16) for h in range(2)]

    def temporal(j):
        cols = slice(j * 128, j * 128 + 128)
        q = got[:, 0, :, cols].reshape(count, 128)
        k = got[:, 1, :, cols].reshape(count, 128)
        v = got[:, 2, :, cols].reshape(count, 128)
        other = (
            lax.broadcasted_iota(jnp.int32, (count, count), 0) % 16
            != lax.broadcasted_iota(jnp.int32, (count, count), 1) % 16
        )
        total = None
        for h in range(2):
            s = mm(q * (sides[h] * jnp.asarray(0.125, bf16)), k, NT)
            s = jnp.where(other, -jnp.inf, s)
            e = jnp.exp(s - jnp.max(s, axis=1, keepdims=True))
            p = (e * (1.0 / jnp.sum(e, axis=1, keepdims=True))).astype(bf16)
            o = mm(p, v * sides[h])
            total = o if total is None else total + o
        back[:, :, cols] = total.astype(bf16).reshape(32, 16, 128)

    for j in range(4):
        temporal(j)

    @pl.loop(1, 32)
    def _(d):
        ret(d).start()

    mine = (pl.ds(pl.multiple_of(seq // 2 * 16, 16), 16), pl.ds(pl.multiple_of(seq % 2 * (width // 2), 128), width // 2))
    frame[mine] = back[seq]

    q_on(2)
    s_on(2)

    def to_partner(ref, unit, yy):
        i = counter[0]
        counter[0] += 1
        span = pl.ds(pl.multiple_of((((y + yy) % 4) * 2 + core) * 4 * unit, 16), 4 * unit)
        c = remote(ref.at[span, :], ref.at[span, :], (w_send, w_recv), i, partner)
        c.start()
        return c

    q_core = [to_partner(wq, 112, yy) for yy in (0, 3, 1)]
    s_end()
    s_core = [to_partner(small, 32, yy) for yy in (0, 3, 1, 2)]
    q_end()
    q_core.append(to_partner(wq, 112, 2))

    @pl.loop(1, 32)
    def _(d):
        ret(d).wait_recv()

    for c in s_core:
        c.wait_recv()
    load_stream.wait()

    halos = []
    part = 64
    for i in range(rows // part):
        span = slice(i * part, (i + 1) * part)
        mixed = (stream[span, :].astype(f32) + mm(frame[span, :], small[:, 0:width])).astype(bf16)
        mixed_out[span, :] = mixed
        for s, d in ((0, 1), (1, 31)):
            c = remote(
                mixed_out.at[span, :], halo.at[s, span, :], (h_send, h_recv), 2 * i + s,
                (grp, (seq + d) % 32),
            )
            c.start()
            halos.append(c)

    def keys_values(b, m):
        for c in range(4):
            cols = slice(c * (width // 2), (c + 1) * (width // 2))
            kv_ref[b * rows : (b + 1) * rows, cols] = mm(m, small[:, width + c * (width // 2) : width + (c + 1) * (width // 2)]).astype(bf16)

    ctx_ref[rows : 2 * rows, :] = mixed_out[...]
    keys_values(1, mixed_out[...])
    for c in q_core:
        c.wait_recv()
    load_text.wait()
    tokens = text.shape[0]
    for i in range(2):
        span = slice(i * (tokens // 2), (i + 1) * (tokens // 2))
        for k in range(2):
            cols = slice(k * (width // 2), (k + 1) * (width // 2))
            q_ref[span, cols] = (mm(text[span, :], wq[:, cols]).astype(bf16) * jnp.asarray(0.125, bf16))
    for c in halos:
        c.wait_recv()
    for s, b in ((0, 0), (1, 2)):
        ctx_ref[b * rows : (b + 1) * rows, :] = halo[s]
        keys_values(b, halo[s])

    for c in halos + q_sent + s_sent + q_core + s_core:
        c.wait_send()

    @pl.loop(1, 32)
    def _(d):
        go(d).wait_send()
        ret(d).wait_send()


def prepare(qkv, wq, wo, wkv, text, stream):
    f32, bf16 = jnp.float32, jnp.bfloat16
    tokens, depth = text.shape
    rows, width = stream.shape
    any_ = pl.BlockSpec(memory_space=pl.ANY)
    dma = pltpu.SemaphoreType.DMA
    return pl.pallas_call(
        prepare_kernel,
        out_shape=(
            jax.ShapeDtypeStruct((tokens, width), bf16),
            jax.ShapeDtypeStruct((3 * rows, width), bf16),
            jax.ShapeDtypeStruct((3 * rows, 2 * width), bf16),
        ),
        in_specs=[any_, VMEM, VMEM, VMEM, any_, any_],
        out_specs=(VMEM, VMEM, VMEM),
        scratch_shapes=[
            pltpu.VMEM((32, width), bf16),
            pltpu.VMEM((16, 2, 3, 16, width // 2), bf16),
            pltpu.VMEM((32, 3, 16, width // 2), bf16),
            pltpu.VMEM((rows, width), bf16),
            pltpu.VMEM((rows, width), bf16),
            pltpu.VMEM((32, 16, width // 2), bf16),
            pltpu.VMEM((tokens, depth), bf16),
            pltpu.VMEM((rows, width), bf16),
            pltpu.VMEM((8, 32, width), bf16),
            pltpu.VMEM((112, width), f32),
            pltpu.VMEM((32, 3 * width), f32),
            pltpu.VMEM((depth, width), bf16),
            pltpu.VMEM((width, 3 * width), bf16),
            pltpu.VMEM((2, rows, width), bf16),
            dma((8,)), dma((8,)), dma((8,)), dma((32,)), dma((32,)), dma((32,)), dma((32,)),
            dma((64,)), dma((64,)), dma((8,)), dma((8,)),
        ],
        compiler_params=pltpu.CompilerParams(
            collective_id=2, has_side_effects=True, vmem_limit_bytes=56 * 2**20
        ),
        name="prepare",
    )(qkv, wq, wo, wkv, text, stream)


def reward_kernel(
    pair_count, mask_ref, label_ref, q_ref, kv, read_ref, ctx_ref, reward_ref, total_ref, grad_ref,
    vt, exps, inverse, d_out_t, d_out, ctx_t, dkv,
    acc, core_out, core_in, a1_out, a1_in, b1_out, b1_in, a2_out, a2_in, b2_out, b2_in,
    a_sum, b_sum, a3_out, a3_in, b3_out, b3_in, z_out, z_in, l_out, l_in, send, recv,
):
    f32, bf16 = jnp.float32, jnp.bfloat16
    tokens, width = q_ref.shape
    rows = kv.shape[0] // 3
    pairs = width // 128
    blocks = [pl.ds(b * rows, rows) for b in range(3)]
    grp, seq = lax.axis_index("grp"), lax.axis_index("seq")
    y, core = grp // 2, grp % 2
    x, z = seq // 8, seq % 8
    half = width // 2
    quarter = half // 2

    def y_peer(d):
        return (((y + d) % 4) * 2 + core, seq)

    def x_peer(d):
        return (grp, ((x + d) % 4) * 8 + z)

    def z_peer(d):
        return (grp, x * 8 + (z + d) % 8)

    partner = (y * 2 + 1 - core, seq)
    peers = [partner] + [y_peer(d) for d in (1, 2, 3)] + [x_peer(d) for d in (1, 2, 3)]
    peers += [z_peer(d) for d in range(1, 8)]
    barrier = pltpu.get_barrier_semaphore()
    for peer in peers:
        pl.semaphore_signal(barrier, inc=1, device_id=peer, device_id_type=MESH)

    count = [0]

    def copy(src, dst, peer):
        i = count[0]
        count[0] += 1
        c = pltpu.make_async_remote_copy(
            src_ref=src, dst_ref=dst, send_sem=send.at[i], recv_sem=recv.at[i],
            device_id=peer, device_id_type=MESH,
        )
        c.start()
        return c

    lane = lax.broadcasted_iota(jnp.int32, (1, 128), 1)
    sides = [((lane // 64) == h).astype(bf16) for h in range(2)]
    bias = [jnp.where(mask_ref[b] == 1, 0.0, -jnp.inf).astype(f32) for b in range(3)]

    def forward(j, squares):
        cols = pl.ds(pl.multiple_of(j * 128, 128), 128)
        vcols = pl.ds(pl.multiple_of(width + j * 128, 128), 128)
        vt[cols, :] = kv[:, vcols].T
        ctx_t[cols, :] = ctx_ref[:, cols].T
        k = kv[:, cols]
        q = q_ref[:, cols]
        for h in range(2):
            s = mm(k, q * sides[h], NT)
            s = [s[b * rows : (b + 1) * rows] for b in range(3)]
            top = [jnp.max(s[b], axis=0, keepdims=True) + bias[b] for b in range(3)]
            top = jnp.maximum(jnp.maximum(top[0], top[1]), top[2])
            total = jnp.zeros((1, tokens), f32)
            for b in range(3):
                e = jnp.exp(s[b] - (top - bias[b]))
                exps[2 * j + h, blocks[b], :] = e
                total = total + jnp.sum(e, axis=0, keepdims=True)
            inv = 1.0 / total
            inverse[2 * j + h] = jnp.broadcast_to(inv, (8, tokens))
            p = (exps[2 * j + h] * inv).astype(bf16)
            mine = pl.ds(pl.multiple_of(j * 128 + h * 64, 64), 64)
            o = mm(vt[mine, :], p)
            acc[j // 4, j % 4, h * 64 : h * 64 + 64, tokens:] = o
            squares = squares + jnp.sum(o * o, axis=0, keepdims=True)
        return squares

    squares = lax.fori_loop(0, pairs, forward, jnp.zeros((1, tokens), f32))
    inv_root = 1.0 / jnp.sqrt(squares / width + EPSILON)

    reward = jnp.zeros((1, tokens), f32)
    inner = jnp.zeros((1, tokens), f32)
    for j in range(pairs):
        normed = acc[j // 4, j % 4, :, tokens:] * inv_root
        gates = jax.nn.sigmoid(normed)
        read = jnp.broadcast_to(read_ref[j : j + 1, :], (128, 128)).T[:, 0:1]
        scaled = read * gates
        slope = scaled * (1.0 + normed * (1.0 - gates))
        acc[j // 4, j % 4, :, 0:tokens] = slope
        reward = reward + jnp.sum(scaled * normed, axis=0, keepdims=True)
        inner = inner + jnp.sum(slope * normed, axis=0, keepdims=True)

    reward = jnp.sum(reward, axis=1, keepdims=True) / tokens
    signed = 2.0 * label_ref[0].astype(f32) - 1.0
    margin = -signed * reward
    loss = jnp.maximum(margin, 0.0) + jnp.log1p(jnp.exp(-jnp.abs(margin)))
    reward_ref[...] = reward
    l_out[0] = jnp.broadcast_to(loss, (8, 128))
    pl.semaphore_wait(barrier, len(peers))
    loss_core = copy(l_out.at[0], l_in.at[0], partner)
    factor = -signed * jax.nn.sigmoid(margin) / pair_count / tokens
    inner = inner / width

    @pl.loop(0, pairs)
    def _(j):
        cols = pl.ds(pl.multiple_of(j * 128, 128), 128)
        normed = acc[j // 4, j % 4, :, tokens:] * inv_root
        d = ((acc[j // 4, j % 4, :, 0:tokens] - normed * inner) * (inv_root * factor)).astype(bf16)
        d_out_t[cols, :] = d
        d_out[:, cols] = d.T

    def backward(j):
        cols = pl.ds(pl.multiple_of(j * 128, 128), 128)
        vcols = pl.ds(pl.multiple_of(width + j * 128, 128), 128)
        v = kv[:, vcols]
        q = q_ref[:, cols]
        do = d_out[:, cols]
        empty = jnp.zeros((64, tokens), bf16)
        dk = dv = None
        for h in range(2):
            mine = d_out_t[pl.ds(pl.multiple_of(j * 128 + h * 64, 64), 64), :]
            mine = jnp.concatenate([mine, empty] if h == 0 else [empty, mine], axis=0)
            dp = mm(v, mine)
            p = exps[2 * j + h] * inverse[2 * j + h, 0:1, :]
            both = p * dp
            ds = (both - p * jnp.sum(both, axis=0, keepdims=True)).astype(bf16)
            dkh = mm(ds, q * sides[h])
            dvh = mm(p.astype(bf16), do * sides[h])
            dk = dkh if dk is None else dk + dkh
            dv = dvh if dv is None else dv + dvh
        place = (j // 4) * width + (j % 4) * 128
        dkv[:, pl.ds(pl.multiple_of(place, 128), 128)] = dk.astype(bf16)
        dkv[:, pl.ds(pl.multiple_of(place + half, 128), 128)] = dv.astype(bf16)

    def chunk(g, yy, side):
        span = pl.ds(pl.multiple_of(((y + yy) % 4) * 256 + side * 128, 128), 128)
        return mm(ctx_t[span, :], dkv[:, g * width : (g + 1) * width])

    def x_rows(d):
        return pl.ds(pl.multiple_of(((x + d) % 4) * 32, 32), 32)

    sent = []
    live = {}

    def begin(g):
        live["core"] = []
        for i in range(4):
            core_out[g, i] = chunk(g, 2 + i, 1 - core).astype(bf16)
            live["core"].append(copy(core_out.at[g, i], core_in.at[g, i], partner))
        for i in range(4):
            acc[g, i] = chunk(g, 2 + i, core)

    def step1(g):
        for c in live["core"]:
            c.wait_recv()
        sent.extend(live["core"])
        acc[g, 0] = acc[g, 0] + core_in[g, 0].astype(f32)
        live["a"], live["b"] = [], []
        for i, d in enumerate((1, 3)):
            a1_out[g, i] = acc[g, 0, :, i * quarter : (i + 1) * quarter].astype(bf16)
            live["a"].append(copy(a1_out.at[g, i], a1_in.at[g, i], y_peer(d)))
        for i in range(1, 4):
            acc[g, i] = acc[g, i] + core_in[g, i].astype(f32)
        for i, d in enumerate((1, 3)):
            cols = slice(half + i * quarter, half + (i + 1) * quarter)
            b1_out[g, i] = acc[g, :, x_rows(2), cols].astype(bf16)
            live["b"].append(copy(b1_out.at[g, i], b1_in.at[g, i], x_peer(d)))

    def step2(g):
        a1, b1 = live["a"], live["b"]
        sent.extend(a1 + b1)
        live["a"], live["b"] = [], []
        for i, d in enumerate((1, 3)):
            lo, hi = slice(i * quarter, (i + 1) * quarter), slice((1 - i) * quarter, (2 - i) * quarter)
            a1[i].wait_recv()
            slot = (3, 1)[i]
            a2_out[g, i, :, lo] = (acc[g, slot, :, lo] + a1_in[g, i].astype(f32)).astype(bf16)
            a2_out[g, i, :, hi] = acc[g, slot, :, hi].astype(bf16)
            live["a"].append(copy(a2_out.at[g, i], a2_in.at[g, i], y_peer(d)))
        for i, d in enumerate((1, 3)):
            lo, hi = slice(i * quarter, (i + 1) * quarter), slice((1 - i) * quarter, (2 - i) * quarter)
            mine = slice(half + i * quarter, half + (i + 1) * quarter)
            rest = slice(half + (1 - i) * quarter, half + (2 - i) * quarter)
            b1[i].wait_recv()
            b2_out[g, i, :, :, lo] = (acc[g, :, x_rows(d), mine] + b1_in[g, i].astype(f32)).astype(bf16)
            b2_out[g, i, :, :, hi] = acc[g, :, x_rows(d), rest].astype(bf16)
            live["b"].append(copy(b2_out.at[g, i], b2_in.at[g, i], x_peer(d)))

    def step3(g):
        a2, b2 = live["a"], live["b"]
        sent.extend(a2 + b2)
        live["a"], live["b"] = [], []
        for c in a2:
            c.wait_recv()
        a_sum[g] = acc[g, 2, :, 0:half] + a2_in[g, 0].astype(f32) + a2_in[g, 1].astype(f32)
        for d in (1, 2, 3):
            a3_out[g, d - 1] = a_sum[g, x_rows(d), :].astype(bf16)
            live["a"].append(copy(a3_out.at[g, d - 1], a3_in.at[g, d - 1], x_peer(d)))
        for c in b2:
            c.wait_recv()
        b_sum[g] = acc[g, :, x_rows(0), half:] + b2_in[g, 0].astype(f32) + b2_in[g, 1].astype(f32)
        for d in (1, 2, 3):
            b3_out[g, d - 1] = b_sum[g, (2 + d) % 4].astype(bf16)
            live["b"].append(copy(b3_out.at[g, d - 1], b3_in.at[g, d - 1], y_peer(d)))

    def step4(g):
        a3, b3 = live["a"], live["b"]
        sent.extend(a3 + b3)
        for c in a3:
            c.wait_recv()
        end = a_sum[g, x_rows(0), :] + (a3_in[g, 0].astype(f32) + a3_in[g, 1].astype(f32) + a3_in[g, 2].astype(f32))
        for i in range(8):
            z_out[g, i, :, 0:half] = end[4 * i : 4 * i + 4]
        for c in b3:
            c.wait_recv()
        end = b_sum[g, 2] + (b3_in[g, 0].astype(f32) + b3_in[g, 1].astype(f32) + b3_in[g, 2].astype(f32))
        for i in range(8):
            z_out[g, i, :, half:] = end[4 * i : 4 * i + 4]
        live["z", g] = [copy(z_out.at[g, (z + d) % 8], z_in.at[g, d - 1], z_peer(d)) for d in range(1, 8)]

    def finish(g):
        sent.extend(live["z", g])
        for c in live["z", g]:
            c.wait_recv()
        grad = z_out[g, z]
        for d in range(1, 8):
            grad = grad + z_in[g, d - 1]
        grad_ref[:, g * half : (g + 1) * half] = grad[:, 0:half]
        grad_ref[:, width + g * half : width + (g + 1) * half] = grad[:, half:]

    def loss_step(before, k, peer_of, ds, slot):
        if not isinstance(before, list):
            before = [before]
        value = l_out[k - 1]
        for i, c in enumerate(before):
            c.wait_recv()
            value = value + l_in[slot + i]
        sent.extend(before)
        l_out[k] = value
        after = slot + len(before)
        return [copy(l_out.at[k], l_in.at[after + i], peer_of(d)) for i, d in enumerate(ds)], after

    @pl.loop(0, 4)
    def _(j):
        backward(j)

    loss_y, slot = loss_step(loss_core, 1, y_peer, (1, 2, 3), 0)
    begin(0)
    backward(4)
    step1(0)
    loss_x, slot = loss_step(loss_y, 2, x_peer, (1, 2, 3), slot)
    backward(5)
    step2(0)
    loss_z, slot = loss_step(loss_x, 3, z_peer, range(1, 8), slot)
    backward(6)
    step3(0)
    backward(7)
    step4(0)
    begin(1)
    total = l_out[3]
    for i, c in enumerate(loss_z):
        c.wait_recv()
        total = total + l_in[slot + i]
    sent.extend(loss_z)
    total_ref[...] = total[0:1, 0:1] / pair_count
    step1(1)
    step2(1)
    finish(0)
    step3(1)
    step4(1)
    finish(1)
    for c in sent:
        c.wait_send()


def reward_and_gradient(mask, label, q, kv, read, ctx, pair_count):
    tokens, width = q.shape
    keys = kv.shape[0]
    f32, bf16 = jnp.float32, jnp.bfloat16
    half, quarter = width // 2, width // 4

    def both(*shape):
        return [pltpu.VMEM((2, *shape), bf16), pltpu.VMEM((2, *shape), bf16)]

    return pl.pallas_call(
        functools.partial(reward_kernel, pair_count),
        out_shape=(
            jax.ShapeDtypeStruct((1, 1), f32),
            jax.ShapeDtypeStruct((1, 1), f32),
            jax.ShapeDtypeStruct((4, 2 * width), f32),
        ),
        in_specs=[SMEM, SMEM] + [VMEM] * 4,
        out_specs=(VMEM, VMEM, VMEM),
        scratch_shapes=[
            pltpu.VMEM((width, keys), bf16),
            pltpu.VMEM((HEADS, keys, tokens), f32),
            pltpu.VMEM((HEADS, 8, tokens), f32),
            pltpu.VMEM((width, tokens), bf16),
            pltpu.VMEM((tokens, width), bf16),
            pltpu.VMEM((width, keys), bf16),
            pltpu.VMEM((keys, 2 * width), bf16),
            pltpu.VMEM((2, 4, 128, width), f32),
            *both(4, 128, width),
            *both(2, 128, quarter),
            *both(2, 4, 32, quarter),
            *both(2, 128, half),
            *both(2, 4, 32, half),
            pltpu.VMEM((2, 128, half), f32),
            pltpu.VMEM((2, 4, 32, half), f32),
            *both(3, 32, half),
            *both(3, 32, half),
            pltpu.VMEM((2, 8, 4, width), f32),
            pltpu.VMEM((2, 7, 4, width), f32),
            pltpu.VMEM((4, 8, 128), f32),
            pltpu.VMEM((14, 8, 128), f32),
            pltpu.SemaphoreType.DMA((64,)),
            pltpu.SemaphoreType.DMA((64,)),
        ],
        compiler_params=pltpu.CompilerParams(
            collective_id=1, has_side_effects=True, vmem_limit_bytes=62 * 2**20
        ),
        name="reward_and_gradient",
    )(mask, label, q, kv, read, ctx)


def local(
    video_stream,
    video_qkv,
    out_weight,
    text_states,
    query_weight,
    kv_weight,
    read_weight,
    block_mask,
    pair_labels,
):
    width = out_weight.shape[1]
    rows = video_stream.shape[2]
    qkv = video_qkv.reshape(rows // 16, 16, 3 * width)
    queries, context, keys_values = prepare(
        qkv, query_weight, out_weight, kv_weight, text_states[0], video_stream.reshape(rows, width)
    )
    pair_count = lax.axis_size("grp") * lax.axis_size("seq")
    reward, loss, kv_grad = reward_and_gradient(
        block_mask[0, 0], pair_labels[0], queries, keys_values, read_weight.reshape(-1, 128), context, pair_count
    )
    return (reward, loss[0, 0], kv_grad)


def solution(mesh):
    placed = (
        P("grp", "seq", None, None),
        P("grp", "seq", None, None),
        P(("grp", "seq"), None),
        P("grp", "seq", None),
        P(("grp", "seq"), None),
        P(("grp", "seq"), None),
        P(),
        P("grp", "seq", None),
        P("grp", "seq"),
    )
    return jax.shard_map(
        local,
        mesh=mesh,
        in_specs=placed,
        out_specs=(P("grp", "seq"), P(), P(("grp", "seq"), None)),
        check_vma=False,
    )
```

```python
import functools
import itertools
import jax
import jax.numpy as jnp
from jax import lax
from jax.experimental import pallas as pl
from jax.experimental.pallas import tpu as pltpu
from jax.sharding import PartitionSpec as P

HEADS = 16
MESH = pl.DeviceIdType.MESH
EPSILON = 1e-06
NN = (((1,), (0,)), ((), ()))
NT = (((1,), (1,)), ((), ()))
VMEM = pl.BlockSpec(memory_space=pltpu.VMEM)
SMEM = pl.BlockSpec(memory_space=pltpu.SMEM)


def mm(a, b, dims=NN):
    return lax.dot_general(a, b, dims, preferred_element_type=jnp.float32)


def prepare_kernel(
    qkv_ref, wq_ref, wo_ref, wkv_ref, text_ref, stream_ref, q_ref, ctx_ref, kv_ref,
    shard, stage, got, mixed_out, frame, back, text, stream, shards, q_tmp, o_tmp, s_tmp, wq, wo, wkv, halo,
    local_sem, z_send, z_recv, go_send, go_recv, ret_send, ret_recv, w_send, w_recv, h_send, h_recv,
):
    f32, bf16 = jnp.float32, jnp.bfloat16
    grp, seq = lax.axis_index("grp"), lax.axis_index("seq")
    y, core = grp // 2, grp % 2
    x, z = seq // 8, seq % 8
    width = wq.shape[1]
    rows = frame.shape[0]
    quarter = width // 4

    def seq_at(d):
        return ((x + d // 8) % 4) * 8 + (z + d % 8) % 8

    def y_peer(d):
        return (((y + d) % 4) * 2 + core, seq)

    def x_peer(d):
        return (grp, ((x + d) % 4) * 8 + z)

    partner = (y * 2 + 1 - core, seq)
    barrier = pltpu.get_barrier_semaphore()

    locals_ = []
    for part in range(3):
        for side in range(4):
            start = part * width + side * quarter
            locals_.append(pltpu.make_async_copy(
                qkv_ref.at[:, :, start : start + quarter], stage.at[:, side // 2, side % 2, part],
                local_sem.at[part * 4 + side],
            ))
    load_text = pltpu.make_async_copy(text_ref, text, local_sem.at[12])
    load_stream = pltpu.make_async_copy(stream_ref, stream, local_sem.at[13])
    for c in locals_ + [load_text, load_stream]:
        c.start()

    @pl.loop(1, 32)
    def _(d):
        pl.semaphore_signal(barrier, inc=1, device_id=(grp, seq_at(d)), device_id_type=MESH)

    for peer in (partner, y_peer(1), y_peer(3)):
        pl.semaphore_signal(barrier, inc=1, device_id=peer, device_id_type=MESH)
    q_tmp[0:14, :] = wq_ref[...].astype(f32)
    q_tmp[16:20, :] = wo_ref[...].astype(f32)
    q_tmp[20:24, :] = wkv_ref[:, 0:width].astype(f32)
    q_tmp[24:28, :] = wkv_ref[:, width:].astype(f32)
    own = q_tmp[0:32, :].astype(bf16)
    shard[...] = own
    shards[z] = own
    pl.semaphore_wait(barrier, 34)

    def remote(src, dst, sems, i, peer):
        return pltpu.make_async_remote_copy(
            src_ref=src, dst_ref=dst, send_sem=sems[0].at[i], recv_sem=sems[1].at[i],
            device_id=peer, device_id_type=MESH,
        )

    def z_copy(d, k):
        span = pl.ds(16 * k, 16)
        return remote(
            shard.at[span, :], shards.at[z, span, :], (z_send, z_recv), 8 * k + d, (grp, x * 8 + (z + d) % 8)
        )

    def go(d, part):
        t = seq_at(d)
        return remote(
            stage.at[t // 2, t % 2, part], got.at[part, seq], (go_send, go_recv), part * 32 + d, (grp, t)
        )

    def home(part):
        first = seq % 2 * (width // 2) + part * quarter
        return (pl.ds(pl.multiple_of(seq // 2 * 16, 16), 16), pl.ds(pl.multiple_of(first, 128), quarter))

    def ret(d, part):
        t = seq_at(d)
        return remote(
            back.at[part, t], frame.at[home(part)], (ret_send, ret_recv), part * 32 + d, (grp, t)
        )

    for k in (1, 0):
        for d in (4, 3, 5, 2, 6, 1, 7):
            z_copy(d, k).start()
    for c in locals_:
        c.wait()

    for part in range(2):

        @pl.loop(1, 32)
        def _(d, part=part):
            go(d, part).start()

        got[part, seq] = stage[seq // 2, seq % 2, part]

    counter = [0]

    def block(unit, yy, xx, lo, n):
        first = (((y + yy) % 4) * 8 + core * 4 + (x + xx) % 4) * unit + lo
        return pl.ds(pl.multiple_of(first, 16), n)

    def spread(ref, unit, cut, first, second, flip):
        at = (lambda a, b, lo, n: block(unit, b, a, lo, n)) if flip else (lambda a, b, lo, n: block(unit, a, b, lo, n))

        def send(a, b, lo, n, peer):
            i = counter[0]
            counter[0] += 1
            span = at(a, b, lo, n)
            c = remote(ref.at[span, :], ref.at[span, :], (w_send, w_recv), i, peer)
            c.start()
            return c

        started = []

        def out(peer_of, a, b):
            pair = [send(a, b, 0, unit, peer_of(1)), send(a, b, 0, unit, peer_of(3))]
            started.extend(pair)
            return pair

        def on(peer_of, a, b, along_first):
            if along_first:
                pair = [send(a - 1, b, 0, cut, peer_of(1)), send(a + 1, b, cut, unit - cut, peer_of(3))]
            else:
                pair = [send(a, b - 1, 0, cut, peer_of(1)), send(a, b + 1, cut, unit - cut, peer_of(3))]
            started.extend(pair)
            return pair

        def arrived(pair):
            for c in pair:
                c.wait_recv()

        state = {}

        def step0():
            state["f"] = out(first, 0, 0)
            state[0] = out(second, 0, 0)

        def step1():
            arrived(state["f"])
            state["ff"] = on(first, 0, 0, True)
            state[3] = out(second, 3, 0)
            state[1] = out(second, 1, 0)

        def step2():
            arrived(state["ff"])
            state[2] = out(second, 2, 0)

        def forward(a):
            arrived(state[a])
            state["s", a] = on(second, a, 0, False)

        def finish():
            for a in range(4):
                arrived(state["s", a])

        return started, step0, step1, step2, forward, finish

    o_sent, o0, o1, o2, o_on, o_end = spread(wo, 32, 16, x_peer, y_peer, True)
    s_sent, s0, s1, s2, s_on, s_end = spread(wkv, 32, 16, y_peer, x_peer, False)
    q_sent, q0, q1, q2, q_on, q_end = spread(wq, 112, 64, x_peer, y_peer, True)

    for d in range(1, 8):
        z_copy(d, 1).wait()
    for i in range(8):
        w = shards[i, 16:32, :].astype(f32)
        o_tmp[4 * i : 4 * i + 4, :] = w[0:4]
        for k in range(2):
            s_tmp[4 * i : 4 * i + 4, k * width : (k + 1) * width] = w[4 + 4 * k : 8 + 4 * k]
    wo[block(32, 0, 0, 0, 32), :] = o_tmp[...].astype(bf16)
    o0()
    wkv[block(32, 0, 0, 0, 32), :] = s_tmp[...].astype(bf16)
    s0()
    for d in range(1, 8):
        z_copy(d, 0).wait()
    for i in range(8):
        q_tmp[14 * i : 14 * i + 14, :] = shards[i, 0:16, :].astype(f32)[0:14]
    wq[block(112, 0, 0, 0, 112), :] = q_tmp[...].astype(bf16)
    q0()
    o1()
    s1()
    q1()
    o2()
    s2()
    q2()
    for a in (0, 3, 1):
        o_on(a)
        q_on(a)
        s_on(a)

    count = 32 * 16
    lane = lax.broadcasted_iota(jnp.int32, (1, 128), 1)
    sides = [((lane // 64) == h).astype(bf16) for h in range(2)]

    def temporal(part, j):
        cols = slice(j * 128, j * 128 + 128)
        q = got[part, :, 0, :, cols].reshape(count, 128)
        k = got[part, :, 1, :, cols].reshape(count, 128)
        v = got[part, :, 2, :, cols].reshape(count, 128)
        other = (
            lax.broadcasted_iota(jnp.int32, (count, count), 0) % 16
            != lax.broadcasted_iota(jnp.int32, (count, count), 1) % 16
        )
        total = None
        for h in range(2):
            s = mm(q * (sides[h] * jnp.asarray(0.125, bf16)), k, NT)
            s = jnp.where(other, -jnp.inf, s)
            e = jnp.exp(s - jnp.max(s, axis=1, keepdims=True))
            p = (e * (1.0 / jnp.sum(e, axis=1, keepdims=True))).astype(bf16)
            o = mm(p, v * sides[h])
            total = o if total is None else total + o
        back[part, :, :, cols] = total.astype(bf16).reshape(32, 16, 128)

    for part in range(2):

        @pl.loop(1, 32)
        def _(d, part=part):
            go(d, part).wait_recv()

        for j in range(2):
            temporal(part, j)

        @pl.loop(1, 32)
        def _(d, part=part):
            ret(d, part).start()

        frame[home(part)] = back[part, seq]

        if part == 0:
            o_on(2)
            s_on(2)
            q_on(2)

    def to_partner(ref, unit, yy):
        i = counter[0]
        counter[0] += 1
        span = pl.ds(pl.multiple_of((((y + yy) % 4) * 2 + core) * 4 * unit, 16), 4 * unit)
        c = remote(ref.at[span, :], ref.at[span, :], (w_send, w_recv), i, partner)
        c.start()
        return c

    o_core = [to_partner(wo, 32, yy) for yy in (0, 3, 1)]
    q_core = [to_partner(wq, 112, yy) for yy in (0, 3, 1)]
    o_end()
    o_core.append(to_partner(wo, 32, 2))
    s_end()
    s_core = [to_partner(wkv, 32, yy) for yy in (0, 3, 1, 2)]

    for part in range(2):

        @pl.loop(1, 32)
        def _(d, part=part):
            ret(d, part).wait_recv()

    for c in o_core:
        c.wait_recv()
    load_stream.wait()

    halos = []
    part = 64
    for i in range(rows // part):
        span = slice(i * part, (i + 1) * part)
        mixed = (stream[span, :].astype(f32) + mm(frame[span, :], wo[...])).astype(bf16)
        mixed_out[span, :] = mixed
        for s, d in ((0, 1), (1, 31)):
            c = remote(
                mixed_out.at[span, :], halo.at[s, span, :], (h_send, h_recv), 2 * i + s,
                (grp, (seq + d) % 32),
            )
            c.start()
            halos.append(c)

    def keys_values(b, m):
        for c in range(4):
            cols = slice(c * (width // 2), (c + 1) * (width // 2))
            kv_ref[b * rows : (b + 1) * rows, cols] = mm(m, wkv[:, cols]).astype(bf16)

    q_end()
    q_core.append(to_partner(wq, 112, 2))
    for c in s_core:
        c.wait_recv()
    ctx_ref[rows : 2 * rows, :] = mixed_out[...]
    keys_values(1, mixed_out[...])
    for c in q_core:
        c.wait_recv()
    load_text.wait()
    tokens = text.shape[0]
    for i in range(2):
        span = slice(i * (tokens // 2), (i + 1) * (tokens // 2))
        for k in range(2):
            cols = slice(k * (width // 2), (k + 1) * (width // 2))
            q_ref[span, cols] = (mm(text[span, :], wq[:, cols]).astype(bf16) * jnp.asarray(0.125, bf16))
    for c in halos:
        c.wait_recv()
    for s, b in ((0, 0), (1, 2)):
        ctx_ref[b * rows : (b + 1) * rows, :] = halo[s]
        keys_values(b, halo[s])

    for c in halos + o_sent + q_sent + s_sent + o_core + q_core + s_core:
        c.wait_send()

    @pl.loop(1, 32)
    def _(d):
        for part in range(2):
            go(d, part).wait_send()
            ret(d, part).wait_send()


def prepare(qkv, wq, wo, wkv, text, stream):
    f32, bf16 = jnp.float32, jnp.bfloat16
    tokens, depth = text.shape
    rows, width = stream.shape
    any_ = pl.BlockSpec(memory_space=pl.ANY)
    dma = pltpu.SemaphoreType.DMA
    return pl.pallas_call(
        prepare_kernel,
        out_shape=(
            jax.ShapeDtypeStruct((tokens, width), bf16),
            jax.ShapeDtypeStruct((3 * rows, width), bf16),
            jax.ShapeDtypeStruct((3 * rows, 2 * width), bf16),
        ),
        in_specs=[any_, VMEM, VMEM, VMEM, any_, any_],
        out_specs=(VMEM, VMEM, VMEM),
        scratch_shapes=[
            pltpu.VMEM((32, width), bf16),
            pltpu.VMEM((16, 2, 2, 3, 16, width // 4), bf16),
            pltpu.VMEM((2, 32, 3, 16, width // 4), bf16),
            pltpu.VMEM((rows, width), bf16),
            pltpu.VMEM((rows, width), bf16),
            pltpu.VMEM((2, 32, 16, width // 4), bf16),
            pltpu.VMEM((tokens, depth), bf16),
            pltpu.VMEM((rows, width), bf16),
            pltpu.VMEM((8, 32, width), bf16),
            pltpu.VMEM((112, width), f32),
            pltpu.VMEM((32, width), f32),
            pltpu.VMEM((32, 2 * width), f32),
            pltpu.VMEM((depth, width), bf16),
            pltpu.VMEM((width, width), bf16),
            pltpu.VMEM((width, 2 * width), bf16),
            pltpu.VMEM((2, rows, width), bf16),
            dma((16,)), dma((16,)), dma((16,)), dma((64,)), dma((64,)), dma((64,)), dma((64,)),
            dma((96,)), dma((96,)), dma((8,)), dma((8,)),
        ],
        compiler_params=pltpu.CompilerParams(
            collective_id=2, has_side_effects=True, vmem_limit_bytes=56 * 2**20
        ),
        name="prepare",
    )(qkv, wq, wo, wkv, text, stream)


PARTS = (4, 3, 1)


def reward_kernel(
    pair_count, mask_ref, label_ref, q_ref, kv, read_ref, ctx_ref, reward_ref, total_ref, grad_ref,
    vt, exps, inverse, d_out_t, d_out, ctx_t, dkv,
    acc, core_out, core_in, a1_out, a1_in, b1_out, b1_in, a_sum, b_sum, a2_out, a2_in, b2_out, b2_in, z_out, z_in, l_out, l_in, send, recv,
):
    f32, bf16 = jnp.float32, jnp.bfloat16
    tokens, width = q_ref.shape
    rows = kv.shape[0] // 3
    pairs = width // 128
    blocks = [pl.ds(b * rows, rows) for b in range(3)]
    grp, seq = lax.axis_index("grp"), lax.axis_index("seq")
    y, core = grp // 2, grp % 2
    x, z = seq // 8, seq % 8
    parts = list(zip((0, *itertools.accumulate(PARTS)), PARTS))

    def y_peer(d):
        return (((y + d) % 4) * 2 + core, seq)

    def x_peer(d):
        return (grp, ((x + d) % 4) * 8 + z)

    def z_peer(d):
        return (grp, x * 8 + (z + d) % 8)

    partner = (y * 2 + 1 - core, seq)
    peers = [partner] + [y_peer(d) for d in (1, 2, 3)] + [x_peer(d) for d in (1, 2, 3)]
    peers += [z_peer(d) for d in range(1, 8)]
    barrier = pltpu.get_barrier_semaphore()
    for peer in peers:
        pl.semaphore_signal(barrier, inc=1, device_id=peer, device_id_type=MESH)

    count = [0]

    def copy(src, dst, peer):
        i = count[0]
        count[0] += 1
        c = pltpu.make_async_remote_copy(
            src_ref=src, dst_ref=dst, send_sem=send.at[i], recv_sem=recv.at[i],
            device_id=peer, device_id_type=MESH,
        )
        c.start()
        return c

    lane = lax.broadcasted_iota(jnp.int32, (1, 128), 1)
    sides = [((lane // 64) == h).astype(bf16) for h in range(2)]
    bias = [jnp.where(mask_ref[b] == 1, 0.0, -jnp.inf).astype(f32) for b in range(3)]

    def forward(j, squares):
        cols = pl.ds(pl.multiple_of(j * 128, 128), 128)
        vcols = pl.ds(pl.multiple_of(width + j * 128, 128), 128)
        vt[cols, :] = kv[:, vcols].T
        ctx_t[cols, :] = ctx_ref[:, cols].T
        k = kv[:, cols]
        q = q_ref[:, cols]
        for h in range(2):
            s = mm(k, q * sides[h], NT)
            s = [s[b * rows : (b + 1) * rows] for b in range(3)]
            top = [jnp.max(s[b], axis=0, keepdims=True) + bias[b] for b in range(3)]
            top = jnp.maximum(jnp.maximum(top[0], top[1]), top[2])
            total = jnp.zeros((1, tokens), f32)
            for b in range(3):
                e = jnp.exp(s[b] - (top - bias[b]))
                exps[2 * j + h, blocks[b], :] = e
                total = total + jnp.sum(e, axis=0, keepdims=True)
            inv = 1.0 / total
            inverse[2 * j + h] = jnp.broadcast_to(inv, (8, tokens))
            p = (exps[2 * j + h] * inv).astype(bf16)
            mine = pl.ds(pl.multiple_of(j * 128 + h * 64, 64), 64)
            o = mm(vt[mine, :], p)
            acc[j % 4, h * 64 : h * 64 + 64, pl.ds(pl.multiple_of((2 + j // 4) * tokens, 128), tokens)] = o
            squares = squares + jnp.sum(o * o, axis=0, keepdims=True)
        return squares

    squares = lax.fori_loop(0, pairs, forward, jnp.zeros((1, tokens), f32))
    inv_root = 1.0 / jnp.sqrt(squares / width + EPSILON)

    reward = jnp.zeros((1, tokens), f32)
    inner = jnp.zeros((1, tokens), f32)
    for j in range(pairs):
        normed = acc[j % 4, :, (2 + j // 4) * tokens : (3 + j // 4) * tokens] * inv_root
        gates = jax.nn.sigmoid(normed)
        read = jnp.broadcast_to(read_ref[j : j + 1, :], (128, 128)).T[:, 0:1]
        scaled = read * gates
        slope = scaled * (1.0 + normed * (1.0 - gates))
        acc[j % 4, :, (j // 4) * tokens : (j // 4 + 1) * tokens] = slope
        reward = reward + jnp.sum(scaled * normed, axis=0, keepdims=True)
        inner = inner + jnp.sum(slope * normed, axis=0, keepdims=True)

    reward = jnp.sum(reward, axis=1, keepdims=True) / tokens
    signed = 2.0 * label_ref[0].astype(f32) - 1.0
    margin = -signed * reward
    loss = jnp.maximum(margin, 0.0) + jnp.log1p(jnp.exp(-jnp.abs(margin)))
    reward_ref[...] = reward
    l_out[0] = jnp.broadcast_to(loss, (8, 128))
    pl.semaphore_wait(barrier, len(peers))
    loss_core = copy(l_out.at[0], l_in.at[0], partner)
    factor = -signed * jax.nn.sigmoid(margin) / pair_count / tokens
    inner = inner / width

    for j in range(pairs):
        cols = slice(j * 128, (j + 1) * 128)
        normed = acc[j % 4, :, (2 + j // 4) * tokens : (3 + j // 4) * tokens] * inv_root
        d = ((acc[j % 4, :, (j // 4) * tokens : (j // 4 + 1) * tokens] - normed * inner) * (inv_root * factor)).astype(bf16)
        d_out_t[cols, :] = d
        d_out[:, cols] = d.T

    def backward(j):
        cols = slice(j * 128, (j + 1) * 128)
        vcols = slice(width + j * 128, width + (j + 1) * 128)
        v = kv[:, vcols]
        q = q_ref[:, cols]
        do = d_out[:, cols]
        empty = jnp.zeros((64, tokens), bf16)
        dk = dv = None
        for h in range(2):
            mine = d_out_t[j * 128 + h * 64 : j * 128 + h * 64 + 64, :]
            mine = jnp.concatenate([mine, empty] if h == 0 else [empty, mine], axis=0)
            dp = mm(v, mine)
            p = exps[2 * j + h] * inverse[2 * j + h, 0:1, :]
            both = p * dp
            ds = (both - p * jnp.sum(both, axis=0, keepdims=True)).astype(bf16)
            dkh = mm(ds, q * sides[h])
            dvh = mm(p.astype(bf16), do * sides[h])
            dk = dkh if dk is None else dk + dkh
            dv = dvh if dv is None else dv + dvh
        first, size = [p for p in parts if p[0] <= j][-1]
        place, half = first * 128 + j * 128, size * 128
        dkv[:, place : place + 128] = dk.astype(bf16)
        dkv[:, place + half : place + half + 128] = dv.astype(bf16)

    def columns(g):
        first, size = parts[g]
        lo, mid, hi = first * 256, first * 256 + size * 128, (first + size) * 256
        return slice(lo, hi), slice(lo, mid), slice(mid, hi), slice(first * 128, (first + size) * 128)

    def chunk(g, yy, side):
        span = pl.ds(pl.multiple_of(((y + yy) % 4) * 256 + side * 128, 128), 128)
        return mm(ctx_t[span, :], dkv[:, columns(g)[0]])

    def x_rows(d):
        return pl.ds(pl.multiple_of(((x + d) % 4) * 32, 32), 32)

    sent = []
    live = {}

    def arrived(name, g):
        sent.extend(live[name, g])
        for c in live[name, g]:
            c.wait_recv()

    def begin(g):
        both = columns(g)[0]
        live["core", g] = []
        for i in range(4):
            core_out[i, :, both] = chunk(g, 2 + i, 1 - core).astype(bf16)
            live["core", g].append(copy(core_out.at[i, :, both], core_in.at[i, :, both], partner))
        for i in range(4):
            acc[i, :, both] = chunk(g, 2 + i, core)

    def step1(g):
        both, a, b, cols = columns(g)
        arrived("core", g)
        for i in range(4):
            acc[i, :, both] = acc[i, :, both] + core_in[i, :, both].astype(f32)
        live["a1", g], live["b1", g] = [], []
        for d in (2, 1, 3):
            a1_out[d - 1, :, cols] = acc[(d + 2) % 4, :, a].astype(bf16)
            live["a1", g].append(copy(a1_out.at[d - 1, :, cols], a1_in.at[d - 1, :, cols], y_peer(d)))
            b1_out[d - 1, :, :, cols] = acc[:, x_rows(d), b].astype(bf16)
            live["b1", g].append(copy(b1_out.at[d - 1, :, :, cols], b1_in.at[d - 1, :, :, cols], x_peer(d)))

    def total_of(ref, cols):
        parts_ = [ref[(d, *[slice(None)] * (len(ref.shape) - 2), cols)].astype(f32) for d in range(3)]
        return parts_[0] + parts_[1] + parts_[2]

    def step2(g):
        both, a, b, cols = columns(g)
        live["a2", g], live["b2", g] = [], []
        arrived("a1", g)
        a_sum[:, cols] = acc[2, :, a] + total_of(a1_in, cols)
        for d in (2, 1, 3):
            a2_out[d - 1, :, cols] = a_sum[x_rows(d), cols].astype(bf16)
            live["a2", g].append(copy(a2_out.at[d - 1, :, cols], a2_in.at[d - 1, :, cols], x_peer(d)))
        arrived("b1", g)
        b_sum[:, :, cols] = acc[:, x_rows(0), b] + total_of(b1_in, cols)
        for d in (2, 1, 3):
            b2_out[d - 1, :, cols] = b_sum[(2 + d) % 4, :, cols].astype(bf16)
            live["b2", g].append(copy(b2_out.at[d - 1, :, cols], b2_in.at[d - 1, :, cols], y_peer(d)))

    def step3(g):
        both, a, b, cols = columns(g)
        arrived("a2", g)
        end = a_sum[x_rows(0), cols] + total_of(a2_in, cols)
        for i in range(8):
            z_out[i, :, a] = end[4 * i : 4 * i + 4]
        arrived("b2", g)
        end = b_sum[2, :, cols] + total_of(b2_in, cols)
        for i in range(8):
            z_out[i, :, b] = end[4 * i : 4 * i + 4]
        live["z", g] = [
            copy(z_out.at[(z + d) % 8, :, both], z_in.at[d - 1, :, both], z_peer(d)) for d in (4, 3, 5, 2, 6, 1, 7)
        ]

    def finish(g):
        both, a, b, cols = columns(g)
        arrived("z", g)
        grad = z_out[z, :, both]
        for d in range(1, 8):
            grad = grad + z_in[d - 1, :, both]
        size = parts[g][1] * 128
        grad_ref[:, cols] = grad[:, 0:size]
        grad_ref[:, width + cols.start : width + cols.stop] = grad[:, size:]

    def loss_step(before, k, peer_of, ds, slot):
        if not isinstance(before, list):
            before = [before]
        value = l_out[k - 1]
        for i, c in enumerate(before):
            c.wait_recv()
            value = value + l_in[slot + i]
        sent.extend(before)
        l_out[k] = value
        after = slot + len(before)
        return [copy(l_out.at[k], l_in.at[after + i], peer_of(d)) for i, d in enumerate(ds)], after

    for j in range(0, 4):
        backward(j)
    loss_y, slot = loss_step(loss_core, 1, y_peer, (1, 2, 3), 0)
    begin(0)
    backward(4)
    step1(0)
    backward(5)
    loss_x, slot = loss_step(loss_y, 2, x_peer, (1, 2, 3), slot)
    backward(6)
    begin(1)
    step2(0)
    step1(1)
    backward(7)
    loss_z, slot = loss_step(loss_x, 3, z_peer, range(1, 8), slot)
    begin(2)
    step3(0)
    step1(2)
    step2(1)
    finish(0)
    step2(2)
    step3(1)
    total = l_out[3]
    for i, c in enumerate(loss_z):
        c.wait_recv()
        total = total + l_in[slot + i]
    sent.extend(loss_z)
    total_ref[...] = total[0:1, 0:1] / pair_count
    step3(2)
    finish(1)
    finish(2)
    for c in sent:
        c.wait_send()


def reward_and_gradient(mask, label, q, kv, read, ctx, pair_count):
    tokens, width = q.shape
    keys = kv.shape[0]
    f32, bf16 = jnp.float32, jnp.bfloat16

    def both(*shape):
        return [pltpu.VMEM(shape, bf16), pltpu.VMEM(shape, bf16)]

    return pl.pallas_call(
        functools.partial(reward_kernel, pair_count),
        out_shape=(
            jax.ShapeDtypeStruct((1, 1), f32),
            jax.ShapeDtypeStruct((1, 1), f32),
            jax.ShapeDtypeStruct((4, 2 * width), f32),
        ),
        in_specs=[SMEM, SMEM] + [VMEM] * 4,
        out_specs=(VMEM, VMEM, VMEM),
        scratch_shapes=[
            pltpu.VMEM((width, keys), bf16),
            pltpu.VMEM((HEADS, keys, tokens), f32),
            pltpu.VMEM((HEADS, 8, tokens), f32),
            pltpu.VMEM((width, tokens), bf16),
            pltpu.VMEM((tokens, width), bf16),
            pltpu.VMEM((width, keys), bf16),
            pltpu.VMEM((keys, 2 * width), bf16),
            pltpu.VMEM((4, 128, 2 * width), f32),
            *both(4, 128, 2 * width),
            *both(3, 128, width),
            *both(3, 4, 32, width),
            pltpu.VMEM((128, width), f32),
            pltpu.VMEM((4, 32, width), f32),
            *both(3, 32, width),
            *both(3, 32, width),
            pltpu.VMEM((8, 4, 2 * width), f32),
            pltpu.VMEM((7, 4, 2 * width), f32),
            pltpu.VMEM((4, 8, 128), f32),
            pltpu.VMEM((14, 8, 128), f32),
            pltpu.SemaphoreType.DMA((128,)),
            pltpu.SemaphoreType.DMA((128,)),
        ],
        compiler_params=pltpu.CompilerParams(
            collective_id=1, has_side_effects=True, vmem_limit_bytes=62 * 2**20
        ),
        name="reward_and_gradient",
    )(mask, label, q, kv, read, ctx)


def local(
    video_stream,
    video_qkv,
    out_weight,
    text_states,
    query_weight,
    kv_weight,
    read_weight,
    block_mask,
    pair_labels,
):
    width = out_weight.shape[1]
    rows = video_stream.shape[2]
    qkv = video_qkv.reshape(rows // 16, 16, 3 * width)
    queries, context, keys_values = prepare(
        qkv, query_weight, out_weight, kv_weight, text_states[0], video_stream.reshape(rows, width)
    )
    pair_count = lax.axis_size("grp") * lax.axis_size("seq")
    reward, loss, kv_grad = reward_and_gradient(
        block_mask[0, 0], pair_labels[0], queries, keys_values, read_weight.reshape(-1, 128), context, pair_count
    )
    return (reward, loss[0, 0], kv_grad)


def solution(mesh):
    placed = (
        P("grp", "seq", None, None),
        P("grp", "seq", None, None),
        P(("grp", "seq"), None),
        P("grp", "seq", None),
        P(("grp", "seq"), None),
        P(("grp", "seq"), None),
        P(),
        P("grp", "seq", None),
        P("grp", "seq"),
    )
    return jax.shard_map(
        local,
        mesh=mesh,
        in_specs=placed,
        out_specs=(P("grp", "seq"), P(), P(("grp", "seq"), None)),
        check_vma=False,
    )
```

```python
import functools
import itertools
import jax
import jax.numpy as jnp
from jax import lax
from jax.experimental import pallas as pl
from jax.experimental.pallas import tpu as pltpu
from jax.sharding import PartitionSpec as P

HEADS = 16
MESH = pl.DeviceIdType.MESH
EPSILON = 1e-06
NN = (((1,), (0,)), ((), ()))
NT = (((1,), (1,)), ((), ()))
VMEM = pl.BlockSpec(memory_space=pltpu.VMEM)
SMEM = pl.BlockSpec(memory_space=pltpu.SMEM)


def mm(a, b, dims=NN):
    return lax.dot_general(a, b, dims, preferred_element_type=jnp.float32)


def prepare_kernel(
    qkv_ref, wq_ref, wo_ref, wkv_ref, text_ref, stream_ref, q_ref, ctx_ref, kv_ref,
    shard, stage, got, mixed_out, frame, back, text, stream, shards, q_tmp, o_tmp, s_tmp, wq, wo, wkv, halo, q_sum, q_out, ctx, kv,
    local_sem, z_send, z_recv, go_send, go_recv, ret_send, ret_recv, w_send, w_recv, h_send, h_recv,
):
    f32, bf16 = jnp.float32, jnp.bfloat16
    grp, seq = lax.axis_index("grp"), lax.axis_index("seq")
    y, core = grp // 2, grp % 2
    x, z = seq // 8, seq % 8
    width = wq.shape[1]
    rows = frame.shape[0]
    quarter = width // 4

    def seq_at(d):
        return ((x + d // 8) % 4) * 8 + (z + d % 8) % 8

    def y_peer(d):
        return (((y + d) % 4) * 2 + core, seq)

    def x_peer(d):
        return (grp, ((x + d) % 4) * 8 + z)

    partner = (y * 2 + 1 - core, seq)
    barrier = pltpu.get_barrier_semaphore()

    locals_ = []
    for part in range(3):
        for side in range(4):
            start = part * width + side * quarter
            locals_.append(pltpu.make_async_copy(
                qkv_ref.at[:, :, start : start + quarter], stage.at[:, side // 2, side % 2, part],
                local_sem.at[part * 4 + side],
            ))
    load_text = pltpu.make_async_copy(text_ref, text, local_sem.at[12])
    load_stream = pltpu.make_async_copy(stream_ref, stream, local_sem.at[13])
    for c in locals_ + [load_text, load_stream]:
        c.start()

    @pl.loop(1, 32)
    def _(d):
        pl.semaphore_signal(barrier, inc=1, device_id=(grp, seq_at(d)), device_id_type=MESH)

    for peer in (partner, y_peer(1), y_peer(3)):
        pl.semaphore_signal(barrier, inc=1, device_id=peer, device_id_type=MESH)
    q_tmp[0:14, :] = wq_ref[...].astype(f32)
    q_tmp[16:20, :] = wo_ref[...].astype(f32)
    q_tmp[20:24, :] = wkv_ref[:, 0:width].astype(f32)
    q_tmp[24:28, :] = wkv_ref[:, width:].astype(f32)
    own = q_tmp[0:32, :].astype(bf16)
    shard[...] = own
    shards[z] = own
    pl.semaphore_wait(barrier, 34)

    def remote(src, dst, sems, i, peer):
        return pltpu.make_async_remote_copy(
            src_ref=src, dst_ref=dst, send_sem=sems[0].at[i], recv_sem=sems[1].at[i],
            device_id=peer, device_id_type=MESH,
        )

    def z_copy(d, k):
        span = pl.ds(16 * k, 16)
        return remote(
            shard.at[span, :], shards.at[z, span, :], (z_send, z_recv), 8 * k + d, (grp, x * 8 + (z + d) % 8)
        )

    def go(d, part):
        t = seq_at(d)
        return remote(
            stage.at[t // 2, t % 2, part], got.at[part, seq], (go_send, go_recv), part * 32 + d, (grp, t)
        )

    def home(part):
        first = seq % 2 * (width // 2) + part * quarter
        return (pl.ds(pl.multiple_of(seq // 2 * 16, 16), 16), pl.ds(pl.multiple_of(first, 128), quarter))

    def ret(d, part):
        t = seq_at(d)
        return remote(
            back.at[part, t], frame.at[home(part)], (ret_send, ret_recv), part * 32 + d, (grp, t)
        )

    for k in (1, 0):
        for d in (4, 3, 5, 2, 6, 1, 7):
            z_copy(d, k).start()
    for c in locals_:
        c.wait()

    for part in range(2):

        @pl.loop(1, 32)
        def _(d, part=part):
            go(d, part).start()

        got[part, seq] = stage[seq // 2, seq % 2, part]

    counter = [0]

    def block(unit, yy, xx, lo, n):
        first = (((y + yy) % 4) * 8 + core * 4 + (x + xx) % 4) * unit + lo
        return pl.ds(pl.multiple_of(first, 16), n)

    def spread(ref, unit, cut, first, second, flip):
        at = (lambda a, b, lo, n: block(unit, b, a, lo, n)) if flip else (lambda a, b, lo, n: block(unit, a, b, lo, n))

        def send(a, b, lo, n, peer):
            i = counter[0]
            counter[0] += 1
            span = at(a, b, lo, n)
            c = remote(ref.at[span, :], ref.at[span, :], (w_send, w_recv), i, peer)
            c.start()
            return c

        started = []

        def out(peer_of, a, b):
            pair = [send(a, b, 0, unit, peer_of(1)), send(a, b, 0, unit, peer_of(3))]
            started.extend(pair)
            return pair

        def on(peer_of, a, b, along_first):
            if along_first:
                pair = [send(a - 1, b, 0, cut, peer_of(1)), send(a + 1, b, cut, unit - cut, peer_of(3))]
            else:
                pair = [send(a, b - 1, 0, cut, peer_of(1)), send(a, b + 1, cut, unit - cut, peer_of(3))]
            started.extend(pair)
            return pair

        def arrived(pair):
            for c in pair:
                c.wait_recv()

        state = {}

        def step0():
            state["f"] = out(first, 0, 0)
            state[0] = out(second, 0, 0)

        def step1():
            arrived(state["f"])
            state["ff"] = on(first, 0, 0, True)
            state[3] = out(second, 3, 0)
            state[1] = out(second, 1, 0)

        def step2():
            arrived(state["ff"])
            state[2] = out(second, 2, 0)

        def forward(a):
            arrived(state[a])
            state["s", a] = on(second, a, 0, False)

        def finish():
            for a in range(4):
                arrived(state["s", a])

        return started, step0, step1, step2, forward, finish

    o_sent, o0, o1, o2, o_on, o_end = spread(wo, 32, 16, x_peer, y_peer, True)
    s_sent, s0, s1, s2, s_on, s_end = spread(wkv, 32, 16, y_peer, x_peer, False)
    q_sent, q0, q1, q2, q_on, q_end = spread(wq, 112, 64, x_peer, y_peer, True)

    for d in range(1, 8):
        z_copy(d, 1).wait()
    for i in range(8):
        w = shards[i, 16:32, :].astype(f32)
        o_tmp[4 * i : 4 * i + 4, :] = w[0:4]
        for k in range(2):
            s_tmp[4 * i : 4 * i + 4, k * width : (k + 1) * width] = w[4 + 4 * k : 8 + 4 * k]
    wo[block(32, 0, 0, 0, 32), :] = o_tmp[...].astype(bf16)
    o0()
    wkv[block(32, 0, 0, 0, 32), :] = s_tmp[...].astype(bf16)
    s0()
    for d in range(1, 8):
        z_copy(d, 0).wait()
    for i in range(8):
        q_tmp[14 * i : 14 * i + 14, :] = shards[i, 0:16, :].astype(f32)[0:14]
    wq[block(112, 0, 0, 0, 112), :] = q_tmp[...].astype(bf16)
    q0()
    o1()
    s1()
    q1()
    o2()
    s2()
    q2()
    for a in (0, 3, 1):
        o_on(a)
        q_on(a)

    count = 32 * 16
    lane = lax.broadcasted_iota(jnp.int32, (1, 128), 1)
    sides = [((lane // 64) == h).astype(bf16) for h in range(2)]

    def temporal(part, j):
        cols = slice(j * 128, j * 128 + 128)
        q = got[part, :, 0, :, cols].reshape(count, 128)
        k = got[part, :, 1, :, cols].reshape(count, 128)
        v = got[part, :, 2, :, cols].reshape(count, 128)
        other = (
            lax.broadcasted_iota(jnp.int32, (count, count), 0) % 16
            != lax.broadcasted_iota(jnp.int32, (count, count), 1) % 16
        )
        total = None
        for h in range(2):
            s = mm(q * (sides[h] * jnp.asarray(0.125, bf16)), k, NT)
            s = jnp.where(other, -jnp.inf, s)
            e = jnp.exp(s - jnp.max(s, axis=1, keepdims=True))
            p = (e * (1.0 / jnp.sum(e, axis=1, keepdims=True))).astype(bf16)
            o = mm(p, v * sides[h])
            total = o if total is None else total + o
        back[part, :, :, cols] = total.astype(bf16).reshape(32, 16, 128)

    for part in range(2):

        @pl.loop(1, 32)
        def _(d, part=part):
            go(d, part).wait_recv()

        for j in range(2):
            temporal(part, j)

        @pl.loop(1, 32)
        def _(d, part=part):
            ret(d, part).start()

        frame[home(part)] = back[part, seq]

        if part == 0:
            s_on(0)
            o_on(2)
            q_on(2)
            s_on(3)
            s_on(1)
        else:
            s_on(2)

    def to_partner(ref, unit, yy):
        i = counter[0]
        counter[0] += 1
        span = pl.ds(pl.multiple_of((((y + yy) % 4) * 2 + core) * 4 * unit, 16), 4 * unit)
        c = remote(ref.at[span, :], ref.at[span, :], (w_send, w_recv), i, partner)
        c.start()
        return c

    o_core = [to_partner(wo, 32, yy) for yy in (0, 3, 1)]
    q_core = [to_partner(wq, 112, yy) for yy in (0, 3, 1)]
    o_end()
    o_core.append(to_partner(wo, 32, 2))
    load_text.wait()
    tokens = text.shape[0]

    def queries(yy):
        span = pl.ds(pl.multiple_of((y + yy) % 4 * 896, 128), 896)
        for k in range(4):
            cols = slice(k * quarter, (k + 1) * quarter)
            part = mm(text[:, span], wq[span, cols])
            if yy == 0:
                q_sum[:, cols] = part
            elif yy == 2:
                q_out[:, cols] = (q_sum[:, cols] + part).astype(bf16) * jnp.asarray(0.125, bf16)
            else:
                q_sum[:, cols] = q_sum[:, cols] + part

    for c, yy in zip(q_core, (0, 3, 1)):
        c.wait_recv()
        queries(yy)

    for c in o_core:
        c.wait_recv()
    load_stream.wait()

    halos = []
    for i, dx in enumerate((0, 1, 2, 3)):
        for part in range(2):

            @pl.loop(max(8 * dx, 1), 8 * dx + 8)
            def _(d, part=part):
                ret(d, part).wait_recv()

        span = pl.ds(pl.multiple_of((x - dx) % 4 * 64, 64), 64)
        mixed = (stream[span, :].astype(f32) + mm(frame[span, :], wo[...])).astype(bf16)
        mixed_out[span, :] = mixed
        for s, d in ((0, 1), (1, 31)):
            c = remote(
                mixed_out.at[span, :], halo.at[s, span, :], (h_send, h_recv), 2 * i + s,
                (grp, (seq + d) % 32),
            )
            c.start()
            halos.append(c)

    def keys_values(b, m):
        for c in range(4):
            cols = slice(c * (width // 2), (c + 1) * (width // 2))
            kv[b * rows : (b + 1) * rows, cols] = mm(m, wkv[:, cols]).astype(bf16)

    s_end()
    s_core = [to_partner(wkv, 32, yy) for yy in (0, 3, 1, 2)]
    q_end()
    q_core.append(to_partner(wq, 112, 2))
    for c in s_core:
        c.wait_recv()
    ctx[rows : 2 * rows, :] = mixed_out[...]
    keys_values(1, mixed_out[...])
    q_core[3].wait_recv()
    queries(2)
    own = slice(rows, 2 * rows)
    saved = [
        pltpu.make_async_copy(q_out, q_ref, local_sem.at[0]),
        pltpu.make_async_copy(ctx.at[own, :], ctx_ref.at[own, :], local_sem.at[1]),
        pltpu.make_async_copy(kv.at[own, :], kv_ref.at[own, :], local_sem.at[2]),
    ]
    for c in saved:
        c.start()
    for c in halos:
        c.wait_recv()
    for s, b in ((0, 0), (1, 2)):
        span = slice(b * rows, (b + 1) * rows)
        ctx[span, :] = halo[s]
        saved.append(pltpu.make_async_copy(ctx.at[span, :], ctx_ref.at[span, :], local_sem.at[3 + 2 * s]))
        saved[-1].start()
        keys_values(b, halo[s])
        saved.append(pltpu.make_async_copy(kv.at[span, :], kv_ref.at[span, :], local_sem.at[4 + 2 * s]))
        saved[-1].start()

    for c in saved:
        c.wait()
    for c in halos + o_sent + q_sent + s_sent + o_core + q_core + s_core:
        c.wait_send()

    @pl.loop(1, 32)
    def _(d):
        for part in range(2):
            go(d, part).wait_send()
            ret(d, part).wait_send()


def prepare(qkv, wq, wo, wkv, text, stream):
    f32, bf16 = jnp.float32, jnp.bfloat16
    tokens, depth = text.shape
    rows, width = stream.shape
    any_ = pl.BlockSpec(memory_space=pl.ANY)
    dma = pltpu.SemaphoreType.DMA
    return pl.pallas_call(
        prepare_kernel,
        out_shape=(
            jax.ShapeDtypeStruct((tokens, width), bf16),
            jax.ShapeDtypeStruct((3 * rows, width), bf16),
            jax.ShapeDtypeStruct((3 * rows, 2 * width), bf16),
        ),
        in_specs=[any_, VMEM, VMEM, VMEM, any_, any_],
        out_specs=(any_, any_, any_),
        scratch_shapes=[
            pltpu.VMEM((32, width), bf16),
            pltpu.VMEM((16, 2, 2, 3, 16, width // 4), bf16),
            pltpu.VMEM((2, 32, 3, 16, width // 4), bf16),
            pltpu.VMEM((rows, width), bf16),
            pltpu.VMEM((rows, width), bf16),
            pltpu.VMEM((2, 32, 16, width // 4), bf16),
            pltpu.VMEM((tokens, depth), bf16),
            pltpu.VMEM((rows, width), bf16),
            pltpu.VMEM((8, 32, width), bf16),
            pltpu.VMEM((112, width), f32),
            pltpu.VMEM((32, width), f32),
            pltpu.VMEM((32, 2 * width), f32),
            pltpu.VMEM((depth, width), bf16),
            pltpu.VMEM((width, width), bf16),
            pltpu.VMEM((width, 2 * width), bf16),
            pltpu.VMEM((2, rows, width), bf16),
            pltpu.VMEM((tokens, width), f32),
            pltpu.VMEM((tokens, width), bf16),
            pltpu.VMEM((3 * rows, width), bf16),
            pltpu.VMEM((3 * rows, 2 * width), bf16),
            dma((16,)), dma((16,)), dma((16,)), dma((64,)), dma((64,)), dma((64,)), dma((64,)),
            dma((96,)), dma((96,)), dma((8,)), dma((8,)),
        ],
        compiler_params=pltpu.CompilerParams(
            collective_id=2, has_side_effects=True, vmem_limit_bytes=56 * 2**20
        ),
        name="prepare",
    )(qkv, wq, wo, wkv, text, stream)


PARTS = (3, 3, 2)


def reward_kernel(
    pair_count, mask_ref, label_ref, q_hbm, kv_hbm, read_ref, ctx_hbm, reward_ref, total_ref, grad_ref,
    q_ref, kv, ctx_ref, load_sem, vt, exps, inverse, d_out_t, d_out, ctx_t, dkv,
    acc, core_out, core_in, a1_out, a1_in, b1_out, b1_in, a_sum, b_sum, a2_out, a2_in, b2_out, b2_in, z_out, z_in, l_out, l_in, send, recv,
):
    f32, bf16 = jnp.float32, jnp.bfloat16
    tokens, width = q_ref.shape
    rows = kv.shape[0] // 3
    pairs = width // 128
    blocks = [pl.ds(b * rows, rows) for b in range(3)]
    grp, seq = lax.axis_index("grp"), lax.axis_index("seq")
    y, core = grp // 2, grp % 2
    x, z = seq // 8, seq % 8
    parts = list(zip((0, *itertools.accumulate(PARTS)), PARTS))

    def y_peer(d):
        return (((y + d) % 4) * 2 + core, seq)

    def x_peer(d):
        return (grp, ((x + d) % 4) * 8 + z)

    def z_peer(d):
        return (grp, x * 8 + (z + d) % 8)

    partner = (y * 2 + 1 - core, seq)
    loads = []
    for k in range(2):
        cols = slice(k * width // 2, (k + 1) * width // 2)
        vcols = slice(width + k * width // 2, width + (k + 1) * width // 2)
        loads.append([
            pltpu.make_async_copy(q_hbm.at[:, cols], q_ref.at[:, cols], load_sem.at[3 * k]),
            pltpu.make_async_copy(kv_hbm.at[:, cols], kv.at[:, cols], load_sem.at[3 * k + 1]),
            pltpu.make_async_copy(kv_hbm.at[:, vcols], kv.at[:, vcols], load_sem.at[3 * k + 2]),
        ])
    loads[1].append(pltpu.make_async_copy(ctx_hbm, ctx_ref, load_sem.at[6]))
    for c in loads[0] + loads[1]:
        c.start()
    peers = [partner] + [y_peer(d) for d in (1, 2, 3)] + [x_peer(d) for d in (1, 2, 3)]
    peers += [z_peer(d) for d in range(1, 8)]
    barrier = pltpu.get_barrier_semaphore()
    for peer in peers:
        pl.semaphore_signal(barrier, inc=1, device_id=peer, device_id_type=MESH)

    count = [0]

    def copy(src, dst, peer):
        i = count[0]
        count[0] += 1
        c = pltpu.make_async_remote_copy(
            src_ref=src, dst_ref=dst, send_sem=send.at[i], recv_sem=recv.at[i],
            device_id=peer, device_id_type=MESH,
        )
        c.start()
        return c

    lane = lax.broadcasted_iota(jnp.int32, (1, 128), 1)
    sides = [((lane // 64) == h).astype(bf16) for h in range(2)]
    bias = [jnp.where(mask_ref[b] == 1, 0.0, -jnp.inf).astype(f32) for b in range(3)]

    def forward(j, squares):
        cols = pl.ds(pl.multiple_of(j * 128, 128), 128)
        vcols = pl.ds(pl.multiple_of(width + j * 128, 128), 128)
        vt[cols, :] = kv[:, vcols].T
        k = kv[:, cols]
        q = q_ref[:, cols]
        for h in range(2):
            s = mm(k, q * sides[h], NT)
            s = [s[b * rows : (b + 1) * rows] for b in range(3)]
            top = [jnp.max(s[b], axis=0, keepdims=True) + bias[b] for b in range(3)]
            top = jnp.maximum(jnp.maximum(top[0], top[1]), top[2])
            total = jnp.zeros((1, tokens), f32)
            for b in range(3):
                e = jnp.exp(s[b] - (top - bias[b]))
                exps[2 * j + h, blocks[b], :] = e
                total = total + jnp.sum(e, axis=0, keepdims=True)
            inv = 1.0 / total
            inverse[2 * j + h] = jnp.broadcast_to(inv, (8, tokens))
            p = (exps[2 * j + h] * inv).astype(bf16)
            mine = pl.ds(pl.multiple_of(j * 128 + h * 64, 64), 64)
            o = mm(vt[mine, :], p)
            acc[j % 4, h * 64 : h * 64 + 64, pl.ds(pl.multiple_of((2 + j // 4) * tokens, 128), tokens)] = o
            squares = squares + jnp.sum(o * o, axis=0, keepdims=True)
        return squares

    squares = jnp.zeros((1, tokens), f32)
    for k in range(2):
        for c in loads[k]:
            c.wait()
        for j in range(k * pairs // 2, (k + 1) * pairs // 2):
            squares = forward(j, squares)
    for j in range(pairs):
        ctx_t[j * 128 : (j + 1) * 128, :] = ctx_ref[:, j * 128 : (j + 1) * 128].T
    inv_root = 1.0 / jnp.sqrt(squares / width + EPSILON)

    reward = jnp.zeros((1, tokens), f32)
    inner = jnp.zeros((1, tokens), f32)
    for j in range(pairs):
        normed = acc[j % 4, :, (2 + j // 4) * tokens : (3 + j // 4) * tokens] * inv_root
        gates = jax.nn.sigmoid(normed)
        read = jnp.broadcast_to(read_ref[j : j + 1, :], (128, 128)).T[:, 0:1]
        scaled = read * gates
        slope = scaled * (1.0 + normed * (1.0 - gates))
        acc[j % 4, :, (j // 4) * tokens : (j // 4 + 1) * tokens] = slope
        reward = reward + jnp.sum(scaled * normed, axis=0, keepdims=True)
        inner = inner + jnp.sum(slope * normed, axis=0, keepdims=True)

    reward = jnp.sum(reward, axis=1, keepdims=True) / tokens
    signed = 2.0 * label_ref[0].astype(f32) - 1.0
    margin = -signed * reward
    loss = jnp.maximum(margin, 0.0) + jnp.log1p(jnp.exp(-jnp.abs(margin)))
    reward_ref[...] = reward
    l_out[0] = jnp.broadcast_to(loss, (8, 128))
    pl.semaphore_wait(barrier, len(peers))
    loss_core = copy(l_out.at[0], l_in.at[0], partner)
    factor = -signed * jax.nn.sigmoid(margin) / pair_count / tokens
    inner = inner / width

    for j in range(pairs):
        cols = slice(j * 128, (j + 1) * 128)
        normed = acc[j % 4, :, (2 + j // 4) * tokens : (3 + j // 4) * tokens] * inv_root
        d = ((acc[j % 4, :, (j // 4) * tokens : (j // 4 + 1) * tokens] - normed * inner) * (inv_root * factor)).astype(bf16)
        d_out_t[cols, :] = d
        d_out[:, cols] = d.T

    def backward(j):
        cols = slice(j * 128, (j + 1) * 128)
        vcols = slice(width + j * 128, width + (j + 1) * 128)
        v = kv[:, vcols]
        q = q_ref[:, cols]
        do = d_out[:, cols]
        empty = jnp.zeros((64, tokens), bf16)
        dk = dv = None
        for h in range(2):
            mine = d_out_t[j * 128 + h * 64 : j * 128 + h * 64 + 64, :]
            mine = jnp.concatenate([mine, empty] if h == 0 else [empty, mine], axis=0)
            dp = mm(v, mine)
            p = exps[2 * j + h] * inverse[2 * j + h, 0:1, :]
            both = p * dp
            ds = (both - p * jnp.sum(both, axis=0, keepdims=True)).astype(bf16)
            dkh = mm(ds, q * sides[h])
            dvh = mm(p.astype(bf16), do * sides[h])
            dk = dkh if dk is None else dk + dkh
            dv = dvh if dv is None else dv + dvh
        first, size = [p for p in parts if p[0] <= j][-1]
        place, half = first * 128 + j * 128, size * 128
        dkv[:, place : place + 128] = dk.astype(bf16)
        dkv[:, place + half : place + half + 128] = dv.astype(bf16)

    def columns(g):
        first, size = parts[g]
        lo, mid, hi = first * 256, first * 256 + size * 128, (first + size) * 256
        return slice(lo, hi), slice(lo, mid), slice(mid, hi), slice(first * 128, (first + size) * 128)

    def chunk(g, yy, side):
        span = pl.ds(pl.multiple_of(((y + yy) % 4) * 256 + side * 128, 128), 128)
        return mm(ctx_t[span, :], dkv[:, columns(g)[0]])

    def x_rows(d):
        return pl.ds(pl.multiple_of(((x + d) % 4) * 32, 32), 32)

    sent = []
    live = {}

    def arrived(name, g):
        sent.extend(live[name, g])
        for c in live[name, g]:
            c.wait_recv()

    def begin(g):
        both = columns(g)[0]
        live["core", g] = []
        for i in range(4):
            core_out[i, :, both] = chunk(g, 2 + i, 1 - core).astype(bf16)
            live["core", g].append(copy(core_out.at[i, :, both], core_in.at[i, :, both], partner))
        for i in range(4):
            acc[i, :, both] = chunk(g, 2 + i, core)

    def step1(g):
        both, a, b, cols = columns(g)
        arrived("core", g)
        for i in range(4):
            acc[i, :, both] = acc[i, :, both] + core_in[i, :, both].astype(f32)
        live["a1", g], live["b1", g] = [], []
        for d in (2, 1, 3):
            a1_out[d - 1, :, cols] = acc[(d + 2) % 4, :, a].astype(bf16)
            live["a1", g].append(copy(a1_out.at[d - 1, :, cols], a1_in.at[d - 1, :, cols], y_peer(d)))
            b1_out[d - 1, :, :, cols] = acc[:, x_rows(d), b].astype(bf16)
            live["b1", g].append(copy(b1_out.at[d - 1, :, :, cols], b1_in.at[d - 1, :, :, cols], x_peer(d)))

    def total_of(ref, cols):
        parts_ = [ref[(d, *[slice(None)] * (len(ref.shape) - 2), cols)].astype(f32) for d in range(3)]
        return parts_[0] + parts_[1] + parts_[2]

    def step2(g):
        both, a, b, cols = columns(g)
        live["a2", g], live["b2", g] = [], []
        arrived("a1", g)
        a_sum[:, cols] = acc[2, :, a] + total_of(a1_in, cols)
        for d in (2, 1, 3):
            a2_out[d - 1, :, cols] = a_sum[x_rows(d), cols].astype(bf16)
            live["a2", g].append(copy(a2_out.at[d - 1, :, cols], a2_in.at[d - 1, :, cols], x_peer(d)))
        arrived("b1", g)
        b_sum[:, :, cols] = acc[:, x_rows(0), b] + total_of(b1_in, cols)
        for d in (2, 1, 3):
            b2_out[d - 1, :, cols] = b_sum[(2 + d) % 4, :, cols].astype(bf16)
            live["b2", g].append(copy(b2_out.at[d - 1, :, cols], b2_in.at[d - 1, :, cols], y_peer(d)))

    def step3(g):
        both, a, b, cols = columns(g)
        arrived("a2", g)
        end = a_sum[x_rows(0), cols] + total_of(a2_in, cols)
        for i in range(8):
            z_out[i, :, a] = end[4 * i : 4 * i + 4]
        arrived("b2", g)
        end = b_sum[2, :, cols] + total_of(b2_in, cols)
        for i in range(8):
            z_out[i, :, b] = end[4 * i : 4 * i + 4]
        live["z", g] = [
            copy(z_out.at[(z + d) % 8, :, both], z_in.at[d - 1, :, both], z_peer(d)) for d in (4, 3, 5, 2, 6, 1, 7)
        ]

    def finish(g):
        both, a, b, cols = columns(g)
        arrived("z", g)
        grad = z_out[z, :, both]
        for d in range(1, 8):
            grad = grad + z_in[d - 1, :, both]
        size = parts[g][1] * 128
        grad_ref[:, cols] = grad[:, 0:size]
        grad_ref[:, width + cols.start : width + cols.stop] = grad[:, size:]

    def loss_step(before, k, peer_of, ds, slot):
        if not isinstance(before, list):
            before = [before]
        value = l_out[k - 1]
        for i, c in enumerate(before):
            c.wait_recv()
            value = value + l_in[slot + i]
        sent.extend(before)
        l_out[k] = value
        after = slot + len(before)
        return [copy(l_out.at[k], l_in.at[after + i], peer_of(d)) for i, d in enumerate(ds)], after

    backward(0)
    backward(1)
    backward(2)
    loss_y, slot = loss_step(loss_core, 1, y_peer, (1, 2, 3), 0)
    begin(0)
    backward(3)
    step1(0)
    backward(4)
    backward(5)
    loss_x, slot = loss_step(loss_y, 2, x_peer, (1, 2, 3), slot)
    begin(1)
    step1(1)
    backward(6)
    step2(0)
    loss_z, slot = loss_step(loss_x, 3, z_peer, range(1, 8), slot)
    backward(7)
    begin(2)
    step1(2)
    step3(0)
    step2(1)
    step2(2)
    step3(1)
    step3(2)
    finish(0)
    total = l_out[3]
    for i, c in enumerate(loss_z):
        c.wait_recv()
        total = total + l_in[slot + i]
    sent.extend(loss_z)
    total_ref[...] = total[0:1, 0:1] / pair_count
    finish(1)
    finish(2)
    for c in sent:
        c.wait_send()


def reward_and_gradient(mask, label, q, kv, read, ctx, pair_count):
    tokens, width = q.shape
    keys = kv.shape[0]
    f32, bf16 = jnp.float32, jnp.bfloat16
    any_ = pl.BlockSpec(memory_space=pl.ANY)

    def both(*shape):
        return [pltpu.VMEM(shape, bf16), pltpu.VMEM(shape, bf16)]

    return pl.pallas_call(
        functools.partial(reward_kernel, pair_count),
        out_shape=(
            jax.ShapeDtypeStruct((1, 1), f32),
            jax.ShapeDtypeStruct((1, 1), f32),
            jax.ShapeDtypeStruct((4, 2 * width), f32),
        ),
        in_specs=[SMEM, SMEM, any_, any_, VMEM, any_],
        out_specs=(VMEM, VMEM, VMEM),
        scratch_shapes=[
            pltpu.VMEM((tokens, width), bf16),
            pltpu.VMEM((keys, 2 * width), bf16),
            pltpu.VMEM((keys, width), bf16),
            pltpu.SemaphoreType.DMA((8,)),
            pltpu.VMEM((width, keys), bf16),
            pltpu.VMEM((HEADS, keys, tokens), f32),
            pltpu.VMEM((HEADS, 8, tokens), f32),
            pltpu.VMEM((width, tokens), bf16),
            pltpu.VMEM((tokens, width), bf16),
            pltpu.VMEM((width, keys), bf16),
            pltpu.VMEM((keys, 2 * width), bf16),
            pltpu.VMEM((4, 128, 2 * width), f32),
            *both(4, 128, 2 * width),
            *both(3, 128, width),
            *both(3, 4, 32, width),
            pltpu.VMEM((128, width), f32),
            pltpu.VMEM((4, 32, width), f32),
            *both(3, 32, width),
            *both(3, 32, width),
            pltpu.VMEM((8, 4, 2 * width), f32),
            pltpu.VMEM((7, 4, 2 * width), f32),
            pltpu.VMEM((4, 8, 128), f32),
            pltpu.VMEM((14, 8, 128), f32),
            pltpu.SemaphoreType.DMA((128,)),
            pltpu.SemaphoreType.DMA((128,)),
        ],
        compiler_params=pltpu.CompilerParams(
            collective_id=1, has_side_effects=True, vmem_limit_bytes=62 * 2**20
        ),
        name="reward_and_gradient",
    )(mask, label, q, kv, read, ctx)


def local(
    video_stream,
    video_qkv,
    out_weight,
    text_states,
    query_weight,
    kv_weight,
    read_weight,
    block_mask,
    pair_labels,
):
    width = out_weight.shape[1]
    rows = video_stream.shape[2]
    qkv = video_qkv.reshape(rows // 16, 16, 3 * width)
    queries, context, keys_values = prepare(
        qkv, query_weight, out_weight, kv_weight, text_states[0], video_stream.reshape(rows, width)
    )
    pair_count = lax.axis_size("grp") * lax.axis_size("seq")
    reward, loss, kv_grad = reward_and_gradient(
        block_mask[0, 0], pair_labels[0], queries, keys_values, read_weight.reshape(-1, 128), context, pair_count
    )
    return (reward, loss[0, 0], kv_grad)


def solution(mesh):
    placed = (
        P("grp", "seq", None, None),
        P("grp", "seq", None, None),
        P(("grp", "seq"), None),
        P("grp", "seq", None),
        P(("grp", "seq"), None),
        P(("grp", "seq"), None),
        P(),
        P("grp", "seq", None),
        P("grp", "seq"),
    )
    return jax.shard_map(
        local,
        mesh=mesh,
        in_specs=placed,
        out_specs=(P("grp", "seq"), P(), P(("grp", "seq"), None)),
        check_vma=False,
    )
```

```python
import functools
import itertools
import jax
import jax.numpy as jnp
from jax import lax
from jax.experimental import pallas as pl
from jax.experimental.pallas import tpu as pltpu
from jax.sharding import PartitionSpec as P

HEADS = 16
MESH = pl.DeviceIdType.MESH
EPSILON = 1e-06
NN = (((1,), (0,)), ((), ()))
NT = (((1,), (1,)), ((), ()))
VMEM = pl.BlockSpec(memory_space=pltpu.VMEM)
SMEM = pl.BlockSpec(memory_space=pltpu.SMEM)


def mm(a, b, dims=NN):
    return lax.dot_general(a, b, dims, preferred_element_type=jnp.float32)


def prepare_kernel(
    qkv_ref, wq_ref, wo_ref, wkv_ref, text_ref, stream_ref, q_ref, ctx_ref, kv_ref,
    shard, stage, got, mixed_out, frame, back, text, stream, shards, q_tmp, o_tmp, s_tmp, wq, wo, wkv, halo, q_sum, q_out, ctx, kv,
    local_sem, z_send, z_recv, go_send, go_recv, ret_send, ret_recv, w_send, w_recv, h_send, h_recv,
):
    f32, bf16 = jnp.float32, jnp.bfloat16
    grp, seq = lax.axis_index("grp"), lax.axis_index("seq")
    y, core = grp // 2, grp % 2
    x, z = seq // 8, seq % 8
    width = wq.shape[1]
    rows = frame.shape[0]
    quarter = width // 4

    def seq_at(d):
        return ((x + d // 8) % 4) * 8 + (z + d % 8) % 8

    def y_peer(d):
        return (((y + d) % 4) * 2 + core, seq)

    def x_peer(d):
        return (grp, ((x + d) % 4) * 8 + z)

    partner = (y * 2 + 1 - core, seq)
    barrier = pltpu.get_barrier_semaphore()

    locals_ = []
    for part in range(3):
        for side in range(4):
            start = part * width + side * quarter
            locals_.append(pltpu.make_async_copy(
                qkv_ref.at[:, :, start : start + quarter], stage.at[:, side // 2, side % 2, part],
                local_sem.at[part * 4 + side],
            ))
    load_text = pltpu.make_async_copy(text_ref, text, local_sem.at[12])
    load_stream = pltpu.make_async_copy(stream_ref, stream, local_sem.at[13])
    for c in locals_ + [load_text, load_stream]:
        c.start()

    @pl.loop(1, 32)
    def _(d):
        pl.semaphore_signal(barrier, inc=1, device_id=(grp, seq_at(d)), device_id_type=MESH)

    for peer in (partner, y_peer(1), y_peer(3)):
        pl.semaphore_signal(barrier, inc=1, device_id=peer, device_id_type=MESH)
    q_tmp[0:14, :] = wq_ref[...].astype(f32)
    q_tmp[16:20, :] = wo_ref[...].astype(f32)
    q_tmp[20:24, :] = wkv_ref[:, 0:width].astype(f32)
    q_tmp[24:28, :] = wkv_ref[:, width:].astype(f32)
    own = q_tmp[0:32, :].astype(bf16)
    shard[...] = own
    shards[z] = own
    pl.semaphore_wait(barrier, 34)

    def remote(src, dst, sems, i, peer):
        return pltpu.make_async_remote_copy(
            src_ref=src, dst_ref=dst, send_sem=sems[0].at[i], recv_sem=sems[1].at[i],
            device_id=peer, device_id_type=MESH,
        )

    def z_copy(d, k):
        span = pl.ds(16 * k, 16)
        return remote(
            shard.at[span, :], shards.at[z, span, :], (z_send, z_recv), 8 * k + d, (grp, x * 8 + (z + d) % 8)
        )

    def go(d, part):
        t = seq_at(d)
        return remote(
            stage.at[t // 2, t % 2, part], got.at[part, seq], (go_send, go_recv), part * 32 + d, (grp, t)
        )

    def home(part):
        first = seq % 2 * (width // 2) + part * quarter
        return (pl.ds(pl.multiple_of(seq // 2 * 16, 16), 16), pl.ds(pl.multiple_of(first, 128), quarter))

    def ret(d, part):
        t = seq_at(d)
        return remote(
            back.at[part, t], frame.at[home(part)], (ret_send, ret_recv), part * 32 + d, (grp, t)
        )

    for k in (1, 0):
        for d in (4, 3, 5, 2, 6, 1, 7):
            z_copy(d, k).start()
    for c in locals_:
        c.wait()

    for part in range(2):

        @pl.loop(1, 32)
        def _(d, part=part):
            go(d, part).start()

        got[part, seq] = stage[seq // 2, seq % 2, part]

    counter = [0]

    def block(unit, yy, xx, lo, n):
        first = (((y + yy) % 4) * 8 + core * 4 + (x + xx) % 4) * unit + lo
        return pl.ds(pl.multiple_of(first, 16), n)

    def spread(ref, unit, cut, first, second, flip):
        at = (lambda a, b, lo, n: block(unit, b, a, lo, n)) if flip else (lambda a, b, lo, n: block(unit, a, b, lo, n))

        def send(a, b, lo, n, peer):
            i = counter[0]
            counter[0] += 1
            span = at(a, b, lo, n)
            c = remote(ref.at[span, :], ref.at[span, :], (w_send, w_recv), i, peer)
            c.start()
            return c

        started = []

        def out(peer_of, a, b):
            pair = [send(a, b, 0, unit, peer_of(1)), send(a, b, 0, unit, peer_of(3))]
            started.extend(pair)
            return pair

        def on(peer_of, a, b, along_first):
            if along_first:
                pair = [send(a - 1, b, 0, cut, peer_of(1)), send(a + 1, b, cut, unit - cut, peer_of(3))]
            else:
                pair = [send(a, b - 1, 0, cut, peer_of(1)), send(a, b + 1, cut, unit - cut, peer_of(3))]
            started.extend(pair)
            return pair

        def arrived(pair):
            for c in pair:
                c.wait_recv()

        state = {}

        def step0():
            state["f"] = out(first, 0, 0)
            state[0] = out(second, 0, 0)

        def step1():
            arrived(state["f"])
            state["ff"] = on(first, 0, 0, True)
            state[3] = out(second, 3, 0)
            state[1] = out(second, 1, 0)

        def step2():
            arrived(state["ff"])
            state[2] = out(second, 2, 0)

        def forward(a):
            arrived(state[a])
            state["s", a] = on(second, a, 0, False)

        def finish():
            for a in range(4):
                arrived(state["s", a])

        return started, step0, step1, step2, forward, finish

    o_sent, o0, o1, o2, o_on, o_end = spread(wo, 32, 16, x_peer, y_peer, True)
    s_sent, s0, s1, s2, s_on, s_end = spread(wkv, 32, 16, y_peer, x_peer, False)
    q_sent, q0, q1, q2, q_on, q_end = spread(wq, 112, 64, x_peer, y_peer, True)

    for d in range(1, 8):
        z_copy(d, 1).wait()
    for i in range(8):
        w = shards[i, 16:32, :].astype(f32)
        o_tmp[4 * i : 4 * i + 4, :] = w[0:4]
        for k in range(2):
            s_tmp[4 * i : 4 * i + 4, k * width : (k + 1) * width] = w[4 + 4 * k : 8 + 4 * k]
    wo[block(32, 0, 0, 0, 32), :] = o_tmp[...].astype(bf16)
    o0()
    wkv[block(32, 0, 0, 0, 32), :] = s_tmp[...].astype(bf16)
    s0()
    for d in range(1, 8):
        z_copy(d, 0).wait()
    for i in range(8):
        q_tmp[14 * i : 14 * i + 14, :] = shards[i, 0:16, :].astype(f32)[0:14]
    wq[block(112, 0, 0, 0, 112), :] = q_tmp[...].astype(bf16)
    q0()
    o1()
    s1()
    q1()
    o2()
    s2()
    q2()
    for a in (0, 3, 1):
        o_on(a)
        q_on(a)

    count = 32 * 16
    lane = lax.broadcasted_iota(jnp.int32, (1, 128), 1)
    sides = [((lane // 64) == h).astype(bf16) for h in range(2)]

    def temporal(part, j):
        cols = slice(j * 128, j * 128 + 128)
        q = got[part, :, 0, :, cols].reshape(count, 128)
        k = got[part, :, 1, :, cols].reshape(count, 128)
        v = got[part, :, 2, :, cols].reshape(count, 128)
        other = (
            lax.broadcasted_iota(jnp.int32, (count, count), 0) % 16
            != lax.broadcasted_iota(jnp.int32, (count, count), 1) % 16
        )
        total = None
        for h in range(2):
            s = mm(q * (sides[h] * jnp.asarray(0.125, bf16)), k, NT)
            s = jnp.where(other, -jnp.inf, s)
            e = jnp.exp(s - jnp.max(s, axis=1, keepdims=True))
            p = (e * (1.0 / jnp.sum(e, axis=1, keepdims=True))).astype(bf16)
            o = mm(p, v * sides[h])
            total = o if total is None else total + o
        back[part, :, :, cols] = total.astype(bf16).reshape(32, 16, 128)

    for part in range(2):

        @pl.loop(1, 32)
        def _(d, part=part):
            go(d, part).wait_recv()

        for j in range(2):
            temporal(part, j)

        @pl.loop(1, 32)
        def _(d, part=part):
            ret(d, part).start()

        frame[home(part)] = back[part, seq]

        if part == 0:
            s_on(0)
            o_on(2)
            q_on(2)
            s_on(3)
            s_on(1)
        else:
            s_on(2)

    def to_partner(ref, unit, yy):
        i = counter[0]
        counter[0] += 1
        span = pl.ds(pl.multiple_of((((y + yy) % 4) * 2 + core) * 4 * unit, 16), 4 * unit)
        c = remote(ref.at[span, :], ref.at[span, :], (w_send, w_recv), i, partner)
        c.start()
        return c

    o_core = [to_partner(wo, 32, yy) for yy in (0, 3, 1)]
    q_core = [to_partner(wq, 112, yy) for yy in (0, 3, 1)]
    o_end()
    o_core.append(to_partner(wo, 32, 2))
    load_text.wait()
    tokens = text.shape[0]

    def queries(yy):
        span = pl.ds(pl.multiple_of((y + yy) % 4 * 896, 128), 896)
        for k in range(4):
            cols = slice(k * quarter, (k + 1) * quarter)
            part = mm(text[:, span], wq[span, cols])
            if yy == 0:
                q_sum[:, cols] = part
            elif yy == 2:
                q_out[:, cols] = (q_sum[:, cols] + part).astype(bf16) * jnp.asarray(0.125, bf16)
            else:
                q_sum[:, cols] = q_sum[:, cols] + part

    for c, yy in zip(q_core, (0, 3, 1)):
        c.wait_recv()
        queries(yy)

    for c in o_core:
        c.wait_recv()
    load_stream.wait()

    halos = []
    for i, dx in enumerate((0, 1, 2, 3)):
        for part in range(2):

            @pl.loop(max(8 * dx, 1), 8 * dx + 8)
            def _(d, part=part):
                ret(d, part).wait_recv()

        span = pl.ds(pl.multiple_of((x - dx) % 4 * 64, 64), 64)
        mixed = (stream[span, :].astype(f32) + mm(frame[span, :], wo[...])).astype(bf16)
        mixed_out[span, :] = mixed
        for s, d in ((0, 1), (1, 31)):
            c = remote(
                mixed_out.at[span, :], halo.at[s, span, :], (h_send, h_recv), 2 * i + s,
                (grp, (seq + d) % 32),
            )
            c.start()
            halos.append(c)

    def keys_values(b, m):
        for c in range(4):
            cols = slice(c * (width // 2), (c + 1) * (width // 2))
            kv[b * rows : (b + 1) * rows, cols] = mm(m, wkv[:, cols]).astype(bf16)

    s_end()
    s_core = [to_partner(wkv, 32, yy) for yy in (0, 3, 1, 2)]
    q_end()
    q_core.append(to_partner(wq, 112, 2))
    for c in s_core:
        c.wait_recv()
    ctx[rows : 2 * rows, :] = mixed_out[...]
    keys_values(1, mixed_out[...])
    q_core[3].wait_recv()
    queries(2)
    own = slice(rows, 2 * rows)
    saved = [
        pltpu.make_async_copy(q_out, q_ref, local_sem.at[0]),
        pltpu.make_async_copy(ctx.at[own, :], ctx_ref.at[own, :], local_sem.at[1]),
        pltpu.make_async_copy(kv.at[own, :], kv_ref.at[own, :], local_sem.at[2]),
    ]
    for c in saved:
        c.start()
    for c in halos:
        c.wait_recv()
    for s, b in ((0, 0), (1, 2)):
        span = slice(b * rows, (b + 1) * rows)
        ctx[span, :] = halo[s]
        saved.append(pltpu.make_async_copy(ctx.at[span, :], ctx_ref.at[span, :], local_sem.at[3 + 2 * s]))
        saved[-1].start()
        keys_values(b, halo[s])
        saved.append(pltpu.make_async_copy(kv.at[span, :], kv_ref.at[span, :], local_sem.at[4 + 2 * s]))
        saved[-1].start()

    for c in saved:
        c.wait()
    for c in halos + o_sent + q_sent + s_sent + o_core + q_core + s_core:
        c.wait_send()

    @pl.loop(1, 32)
    def _(d):
        for part in range(2):
            go(d, part).wait_send()
            ret(d, part).wait_send()


def prepare(qkv, wq, wo, wkv, text, stream):
    f32, bf16 = jnp.float32, jnp.bfloat16
    tokens, depth = text.shape
    rows, width = stream.shape
    any_ = pl.BlockSpec(memory_space=pl.ANY)
    dma = pltpu.SemaphoreType.DMA
    return pl.pallas_call(
        prepare_kernel,
        out_shape=(
            jax.ShapeDtypeStruct((tokens, width), bf16),
            jax.ShapeDtypeStruct((3 * rows, width), bf16),
            jax.ShapeDtypeStruct((3 * rows, 2 * width), bf16),
        ),
        in_specs=[any_, VMEM, VMEM, VMEM, any_, any_],
        out_specs=(any_, any_, any_),
        scratch_shapes=[
            pltpu.VMEM((32, width), bf16),
            pltpu.VMEM((16, 2, 2, 3, 16, width // 4), bf16),
            pltpu.VMEM((2, 32, 3, 16, width // 4), bf16),
            pltpu.VMEM((rows, width), bf16),
            pltpu.VMEM((rows, width), bf16),
            pltpu.VMEM((2, 32, 16, width // 4), bf16),
            pltpu.VMEM((tokens, depth), bf16),
            pltpu.VMEM((rows, width), bf16),
            pltpu.VMEM((8, 32, width), bf16),
            pltpu.VMEM((112, width), f32),
            pltpu.VMEM((32, width), f32),
            pltpu.VMEM((32, 2 * width), f32),
            pltpu.VMEM((depth, width), bf16),
            pltpu.VMEM((width, width), bf16),
            pltpu.VMEM((width, 2 * width), bf16),
            pltpu.VMEM((2, rows, width), bf16),
            pltpu.VMEM((tokens, width), f32),
            pltpu.VMEM((tokens, width), bf16),
            pltpu.VMEM((3 * rows, width), bf16),
            pltpu.VMEM((3 * rows, 2 * width), bf16),
            dma((16,)), dma((16,)), dma((16,)), dma((64,)), dma((64,)), dma((64,)), dma((64,)),
            dma((96,)), dma((96,)), dma((8,)), dma((8,)),
        ],
        compiler_params=pltpu.CompilerParams(
            collective_id=2, has_side_effects=True, vmem_limit_bytes=56 * 2**20
        ),
        name="prepare",
    )(qkv, wq, wo, wkv, text, stream)


PARTS = (3, 3, 2)


def reward_kernel(
    pair_count, mask_ref, label_ref, q_hbm, kv_hbm, read_ref, ctx_hbm, reward_ref, total_ref, grad_ref,
    q_ref, kv, ctx_ref, load_sem, vt, exps, inverse, d_out_t, d_out, ctx_t, dkv,
    acc, core_out, core_in, a1_out, a1_in, b1_out, b1_in, a_sum, b_sum, a2_out, a2_in, b2_out, b2_in, z_out, z_in, l_out, l_in, send, recv,
):
    f32, bf16 = jnp.float32, jnp.bfloat16
    tokens, width = q_ref.shape
    rows = kv.shape[0] // 3
    pairs = width // 128
    blocks = [pl.ds(b * rows, rows) for b in range(3)]
    grp, seq = lax.axis_index("grp"), lax.axis_index("seq")
    y, core = grp // 2, grp % 2
    x, z = seq // 8, seq % 8
    parts = list(zip((0, *itertools.accumulate(PARTS)), PARTS))

    def y_peer(d):
        return (((y + d) % 4) * 2 + core, seq)

    def x_peer(d):
        return (grp, ((x + d) % 4) * 8 + z)

    def z_peer(d):
        return (grp, x * 8 + (z + d) % 8)

    partner = (y * 2 + 1 - core, seq)
    loads = []
    for k in range(2):
        cols = slice(k * width // 2, (k + 1) * width // 2)
        vcols = slice(width + k * width // 2, width + (k + 1) * width // 2)
        loads.append([
            pltpu.make_async_copy(q_hbm.at[:, cols], q_ref.at[:, cols], load_sem.at[3 * k]),
            pltpu.make_async_copy(kv_hbm.at[:, cols], kv.at[:, cols], load_sem.at[3 * k + 1]),
            pltpu.make_async_copy(kv_hbm.at[:, vcols], kv.at[:, vcols], load_sem.at[3 * k + 2]),
        ])
    loads[1].append(pltpu.make_async_copy(ctx_hbm, ctx_ref, load_sem.at[6]))
    for c in loads[0] + loads[1]:
        c.start()
    peers = [partner] + [y_peer(d) for d in (1, 2, 3)] + [x_peer(d) for d in (1, 2, 3)]
    peers += [z_peer(d) for d in range(1, 8)]
    barrier = pltpu.get_barrier_semaphore()
    for peer in peers:
        pl.semaphore_signal(barrier, inc=1, device_id=peer, device_id_type=MESH)

    count = [0]

    def copy(src, dst, peer):
        i = count[0]
        count[0] += 1
        c = pltpu.make_async_remote_copy(
            src_ref=src, dst_ref=dst, send_sem=send.at[i], recv_sem=recv.at[i],
            device_id=peer, device_id_type=MESH,
        )
        c.start()
        return c

    lane = lax.broadcasted_iota(jnp.int32, (1, 128), 1)
    sides = [((lane // 64) == h).astype(bf16) for h in range(2)]
    bias = [jnp.where(mask_ref[b] == 1, 0.0, -jnp.inf).astype(f32) for b in range(3)]

    def forward(j, squares):
        cols = pl.ds(pl.multiple_of(j * 128, 128), 128)
        vcols = pl.ds(pl.multiple_of(width + j * 128, 128), 128)
        vt[cols, :] = kv[:, vcols].T
        k = kv[:, cols]
        q = q_ref[:, cols]
        for h in range(2):
            s = mm(k, q * sides[h], NT)
            s = [s[b * rows : (b + 1) * rows] for b in range(3)]
            top = [jnp.max(s[b], axis=0, keepdims=True) + bias[b] for b in range(3)]
            top = jnp.maximum(jnp.maximum(top[0], top[1]), top[2])
            total = jnp.zeros((1, tokens), f32)
            for b in range(3):
                e = jnp.exp(s[b] - (top - bias[b]))
                exps[2 * j + h, blocks[b], :] = e
                total = total + jnp.sum(e, axis=0, keepdims=True)
            inv = 1.0 / total
            inverse[2 * j + h] = jnp.broadcast_to(inv, (8, tokens))
            p = (exps[2 * j + h] * inv).astype(bf16)
            mine = pl.ds(pl.multiple_of(j * 128 + h * 64, 64), 64)
            o = mm(vt[mine, :], p)
            acc[j % 4, h * 64 : h * 64 + 64, pl.ds(pl.multiple_of((2 + j // 4) * tokens, 128), tokens)] = o
            squares = squares + jnp.sum(o * o, axis=0, keepdims=True)
        return squares

    squares = jnp.zeros((1, tokens), f32)
    for k in range(2):
        for c in loads[k]:
            c.wait()
        squares = lax.fori_loop(k * pairs // 2, (k + 1) * pairs // 2, forward, squares)

    @pl.loop(0, pairs)
    def _(j):
        cols = pl.ds(pl.multiple_of(j * 128, 128), 128)
        ctx_t[cols, :] = ctx_ref[:, cols].T

    inv_root = 1.0 / jnp.sqrt(squares / width + EPSILON)

    reward = jnp.zeros((1, tokens), f32)
    inner = jnp.zeros((1, tokens), f32)
    for j in range(pairs):
        normed = acc[j % 4, :, (2 + j // 4) * tokens : (3 + j // 4) * tokens] * inv_root
        gates = jax.nn.sigmoid(normed)
        read = jnp.broadcast_to(read_ref[j : j + 1, :], (128, 128)).T[:, 0:1]
        scaled = read * gates
        slope = scaled * (1.0 + normed * (1.0 - gates))
        acc[j % 4, :, (j // 4) * tokens : (j // 4 + 1) * tokens] = slope
        reward = reward + jnp.sum(scaled * normed, axis=0, keepdims=True)
        inner = inner + jnp.sum(slope * normed, axis=0, keepdims=True)

    reward = jnp.sum(reward, axis=1, keepdims=True) / tokens
    signed = 2.0 * label_ref[0].astype(f32) - 1.0
    margin = -signed * reward
    loss = jnp.maximum(margin, 0.0) + jnp.log1p(jnp.exp(-jnp.abs(margin)))
    reward_ref[...] = reward
    l_out[0] = jnp.broadcast_to(loss, (8, 128))
    pl.semaphore_wait(barrier, len(peers))
    loss_core = copy(l_out.at[0], l_in.at[0], partner)
    factor = -signed * jax.nn.sigmoid(margin) / pair_count / tokens
    inner = inner / width

    for j in range(pairs):
        cols = slice(j * 128, (j + 1) * 128)
        normed = acc[j % 4, :, (2 + j // 4) * tokens : (3 + j // 4) * tokens] * inv_root
        d = ((acc[j % 4, :, (j // 4) * tokens : (j // 4 + 1) * tokens] - normed * inner) * (inv_root * factor)).astype(bf16)
        d_out_t[cols, :] = d
        d_out[:, cols] = d.T

    def backward(j, part):
        cols = pl.ds(pl.multiple_of(j * 128, 128), 128)
        vcols = pl.ds(pl.multiple_of(width + j * 128, 128), 128)
        v = kv[:, vcols]
        q = q_ref[:, cols]
        do = d_out[:, cols]
        empty = jnp.zeros((64, tokens), bf16)
        dk = dv = None
        for h in range(2):
            mine = d_out_t[pl.ds(pl.multiple_of(j * 128 + h * 64, 64), 64), :]
            mine = jnp.concatenate([mine, empty] if h == 0 else [empty, mine], axis=0)
            dp = mm(v, mine)
            p = exps[2 * j + h] * inverse[2 * j + h, 0:1, :]
            both = p * dp
            ds = (both - p * jnp.sum(both, axis=0, keepdims=True)).astype(bf16)
            dkh = mm(ds, q * sides[h])
            dvh = mm(p.astype(bf16), do * sides[h])
            dk = dkh if dk is None else dk + dkh
            dv = dvh if dv is None else dv + dvh
        first, size = parts[part]
        place, half = pl.multiple_of(first * 128 + j * 128, 128), size * 128
        dkv[:, pl.ds(place, 128)] = dk.astype(bf16)
        dkv[:, pl.ds(pl.multiple_of(place + half, 128), 128)] = dv.astype(bf16)

    def columns(g):
        first, size = parts[g]
        lo, mid, hi = first * 256, first * 256 + size * 128, (first + size) * 256
        return slice(lo, hi), slice(lo, mid), slice(mid, hi), slice(first * 128, (first + size) * 128)

    def chunk(g, yy, side):
        span = pl.ds(pl.multiple_of(((y + yy) % 4) * 256 + side * 128, 128), 128)
        return mm(ctx_t[span, :], dkv[:, columns(g)[0]])

    def x_rows(d):
        return pl.ds(pl.multiple_of(((x + d) % 4) * 32, 32), 32)

    sent = []
    live = {}

    def arrived(name, g):
        sent.extend(live[name, g])
        for c in live[name, g]:
            c.wait_recv()

    def begin(g):
        both = columns(g)[0]
        live["core", g] = []
        for i in range(4):
            core_out[i, :, both] = chunk(g, 2 + i, 1 - core).astype(bf16)
            live["core", g].append(copy(core_out.at[i, :, both], core_in.at[i, :, both], partner))
        for i in range(4):
            acc[i, :, both] = chunk(g, 2 + i, core)

    def step1(g):
        both, a, b, cols = columns(g)
        arrived("core", g)
        for i in range(4):
            acc[i, :, both] = acc[i, :, both] + core_in[i, :, both].astype(f32)
        live["a1", g], live["b1", g] = [], []
        for d in (2, 1, 3):
            a1_out[d - 1, :, cols] = acc[(d + 2) % 4, :, a].astype(bf16)
            live["a1", g].append(copy(a1_out.at[d - 1, :, cols], a1_in.at[d - 1, :, cols], y_peer(d)))
            b1_out[d - 1, :, :, cols] = acc[:, x_rows(d), b].astype(bf16)
            live["b1", g].append(copy(b1_out.at[d - 1, :, :, cols], b1_in.at[d - 1, :, :, cols], x_peer(d)))

    def total_of(ref, cols):
        parts_ = [ref[(d, *[slice(None)] * (len(ref.shape) - 2), cols)].astype(f32) for d in range(3)]
        return parts_[0] + parts_[1] + parts_[2]

    def step2(g):
        both, a, b, cols = columns(g)
        live["a2", g], live["b2", g] = [], []
        arrived("a1", g)
        a_sum[:, cols] = acc[2, :, a] + total_of(a1_in, cols)
        for d in (2, 1, 3):
            a2_out[d - 1, :, cols] = a_sum[x_rows(d), cols].astype(bf16)
            live["a2", g].append(copy(a2_out.at[d - 1, :, cols], a2_in.at[d - 1, :, cols], x_peer(d)))
        arrived("b1", g)
        b_sum[:, :, cols] = acc[:, x_rows(0), b] + total_of(b1_in, cols)
        for d in (2, 1, 3):
            b2_out[d - 1, :, cols] = b_sum[(2 + d) % 4, :, cols].astype(bf16)
            live["b2", g].append(copy(b2_out.at[d - 1, :, cols], b2_in.at[d - 1, :, cols], y_peer(d)))

    def step3(g):
        both, a, b, cols = columns(g)
        arrived("a2", g)
        end = a_sum[x_rows(0), cols] + total_of(a2_in, cols)
        for i in range(8):
            z_out[i, :, a] = end[4 * i : 4 * i + 4]
        arrived("b2", g)
        end = b_sum[2, :, cols] + total_of(b2_in, cols)
        for i in range(8):
            z_out[i, :, b] = end[4 * i : 4 * i + 4]
        live["z", g] = [
            copy(z_out.at[(z + d) % 8, :, both], z_in.at[d - 1, :, both], z_peer(d)) for d in (4, 3, 5, 2, 6, 1, 7)
        ]

    def finish(g):
        both, a, b, cols = columns(g)
        arrived("z", g)
        grad = z_out[z, :, both]
        for d in range(1, 8):
            grad = grad + z_in[d - 1, :, both]
        size = parts[g][1] * 128
        grad_ref[:, cols] = grad[:, 0:size]
        grad_ref[:, width + cols.start : width + cols.stop] = grad[:, size:]

    def loss_step(before, k, peer_of, ds, slot):
        if not isinstance(before, list):
            before = [before]
        value = l_out[k - 1]
        for i, c in enumerate(before):
            c.wait_recv()
            value = value + l_in[slot + i]
        sent.extend(before)
        l_out[k] = value
        after = slot + len(before)
        return [copy(l_out.at[k], l_in.at[after + i], peer_of(d)) for i, d in enumerate(ds)], after

    @pl.loop(0, 3)
    def _(j):
        backward(j, 0)

    loss_y, slot = loss_step(loss_core, 1, y_peer, (1, 2, 3), 0)
    begin(0)
    backward(3, 1)
    step1(0)
    backward(4, 1)
    backward(5, 1)
    loss_x, slot = loss_step(loss_y, 2, x_peer, (1, 2, 3), slot)
    begin(1)
    step1(1)
    backward(6, 2)
    step2(0)
    loss_z, slot = loss_step(loss_x, 3, z_peer, range(1, 8), slot)
    backward(7, 2)
    begin(2)
    step1(2)
    step3(0)
    step2(1)
    step2(2)
    step3(1)
    step3(2)
    finish(0)
    total = l_out[3]
    for i, c in enumerate(loss_z):
        c.wait_recv()
        total = total + l_in[slot + i]
    sent.extend(loss_z)
    total_ref[...] = total[0:1, 0:1] / pair_count
    finish(1)
    finish(2)
    for c in sent:
        c.wait_send()


def reward_and_gradient(mask, label, q, kv, read, ctx, pair_count):
    tokens, width = q.shape
    keys = kv.shape[0]
    f32, bf16 = jnp.float32, jnp.bfloat16
    any_ = pl.BlockSpec(memory_space=pl.ANY)

    def both(*shape):
        return [pltpu.VMEM(shape, bf16), pltpu.VMEM(shape, bf16)]

    return pl.pallas_call(
        functools.partial(reward_kernel, pair_count),
        out_shape=(
            jax.ShapeDtypeStruct((1, 1), f32),
            jax.ShapeDtypeStruct((1, 1), f32),
            jax.ShapeDtypeStruct((4, 2 * width), f32),
        ),
        in_specs=[SMEM, SMEM, any_, any_, VMEM, any_],
        out_specs=(VMEM, VMEM, VMEM),
        scratch_shapes=[
            pltpu.VMEM((tokens, width), bf16),
            pltpu.VMEM((keys, 2 * width), bf16),
            pltpu.VMEM((keys, width), bf16),
            pltpu.SemaphoreType.DMA((8,)),
            pltpu.VMEM((width, keys), bf16),
            pltpu.VMEM((HEADS, keys, tokens), f32),
            pltpu.VMEM((HEADS, 8, tokens), f32),
            pltpu.VMEM((width, tokens), bf16),
            pltpu.VMEM((tokens, width), bf16),
            pltpu.VMEM((width, keys), bf16),
            pltpu.VMEM((keys, 2 * width), bf16),
            pltpu.VMEM((4, 128, 2 * width), f32),
            *both(4, 128, 2 * width),
            *both(3, 128, width),
            *both(3, 4, 32, width),
            pltpu.VMEM((128, width), f32),
            pltpu.VMEM((4, 32, width), f32),
            *both(3, 32, width),
            *both(3, 32, width),
            pltpu.VMEM((8, 4, 2 * width), f32),
            pltpu.VMEM((7, 4, 2 * width), f32),
            pltpu.VMEM((4, 8, 128), f32),
            pltpu.VMEM((14, 8, 128), f32),
            pltpu.SemaphoreType.DMA((128,)),
            pltpu.SemaphoreType.DMA((128,)),
        ],
        compiler_params=pltpu.CompilerParams(
            collective_id=1, has_side_effects=True, vmem_limit_bytes=62 * 2**20
        ),
        name="reward_and_gradient",
    )(mask, label, q, kv, read, ctx)


def local(
    video_stream,
    video_qkv,
    out_weight,
    text_states,
    query_weight,
    kv_weight,
    read_weight,
    block_mask,
    pair_labels,
):
    width = out_weight.shape[1]
    rows = video_stream.shape[2]
    qkv = video_qkv.reshape(rows // 16, 16, 3 * width)
    queries, context, keys_values = prepare(
        qkv, query_weight, out_weight, kv_weight, text_states[0], video_stream.reshape(rows, width)
    )
    pair_count = lax.axis_size("grp") * lax.axis_size("seq")
    reward, loss, kv_grad = reward_and_gradient(
        block_mask[0, 0], pair_labels[0], queries, keys_values, read_weight.reshape(-1, 128), context, pair_count
    )
    return (reward, loss[0, 0], kv_grad)


def solution(mesh):
    placed = (
        P("grp", "seq", None, None),
        P("grp", "seq", None, None),
        P(("grp", "seq"), None),
        P("grp", "seq", None),
        P(("grp", "seq"), None),
        P(("grp", "seq"), None),
        P(),
        P("grp", "seq", None),
        P("grp", "seq"),
    )
    return jax.shard_map(
        local,
        mesh=mesh,
        in_specs=placed,
        out_specs=(P("grp", "seq"), P(), P(("grp", "seq"), None)),
        check_vma=False,
    )
```
